256 devices in a mesh: day: 32 (over y, x, core), cls: 8 (over z).
Axes of the slice: x: 4, y: 4, z: 8, core: 2. Of those that a mesh axis runs over, the one named last changes fastest.
Arguments:
- cost: float32 [256, 8, 65536], P('day', None, 'cls'), may hold values from -6 to 6
- x_start: float32 [256, 8, 65536], P('day', None, 'cls'), may hold values from 0 to 1
- ybal_start: float32 [256, 65536], P('day', 'cls'), may hold values from -3 to 3
- inflow: float32 [256, 65536], P('day', 'cls'), may hold values from 0.5 to 3
- ycap_start: float32 [256, 256], P('day', 'cls'), may hold values from -1 to 0
- capacity: float32 [256, 256], P('day', 'cls'), may hold values from 2 to 60
- upper: float32 [8, 65536], P(None, 'cls'), may hold values from 0.3 to 3
- facility: int32 [65536], P('cls'), may hold values from 0 to 255
- option_count: int32 [65536], P('cls'), may hold values from 1 to 8
- decay_index: int32 [65536], P('cls'), may hold values from 0 to 15
- decay_table: float32 [16], replicated, may hold values from 0.3 to 0.99
- usage: float32 [8], replicated, may hold values from 0.02 to 0.2
Outputs:
- x_final: float32 [256, 8, 65536], P('day', None, 'cls')
- ybal_final: float32 [256, 65536], P('day', 'cls')
- ycap_final: float32 [256, 256], P('day', 'cls')
The draws below stay inside these ranges and needn't reach their ends.
All inputs are finite; a program needn't handle non-finite values.
Results may differ from the reference program's by a relative error of at most 0.0003.
Values sent between devices are 32-bit elements; how exact they have to be, the bound alone decides.
No kernel may reach another device: no remote copies, remote signals or barrier semaphores. Data moves between devices by JAX's collectives and lax.ppermute only.
A program may use at most 64 MiB of HBM per device.

```python
import math
import jax
import jax.numpy as jnp
import numpy as np
from jax import lax

OPT = 8
LEVELS = 16
ITERS = 2
DAYS = 256
CLASSES = 65536
FACILITIES = 256


def with_ends(drawn, key, smallest, top_value):
    spot = [jax.random.randint(jax.random.fold_in(key, axis), (), 0, length) for axis, length in enumerate(drawn.shape)]
    longest = drawn.shape.index(max(drawn.shape))
    neighbour = spot[:longest] + [(spot[longest] + 1) % drawn.shape[longest]] + spot[longest + 1:]
    return drawn.at[tuple(spot)].set(smallest).at[tuple(neighbour)].set(top_value)


def shard_levels(own_key, shape, cuts, low, high):
    def one(position, blocks):
        draws = jax.random.uniform(jax.random.fold_in(jax.random.fold_in(own_key, 6), position), (blocks,), jnp.float32, low / len(cuts), high / len(cuts))
        return jnp.repeat(jnp.exp(draws), shape[position] // blocks).reshape((-1,) + (1,) * (len(shape) - position - 1))

    factor_of = one(*cuts[0])
    for cut in cuts[1:]:
        factor_of = factor_of * one(*cut)
    return factor_of


def rank_table(count, slope):
    weights = [(1 << 20) // math.isqrt(grade ** slope) + 1 for grade in range(1, count + 1)]
    scale = 1 + sum(weights) // (1 << 30)
    return np.cumsum(np.array([max(1, weight // scale) for weight in weights]))


def skewed_ids(rng, dims, count, slope):
    table = rank_table(count, slope)
    lot = jax.random.randint(jax.random.fold_in(rng, 1), dims, 0, int(table[count - 1]))
    rank = jnp.searchsorted(jnp.asarray(table, jnp.int32), lot, side="right")
    return jax.random.permutation(jax.random.fold_in(rng, 2), count)[rank].astype(jnp.int32)


def gaussian(own_key, extent, width, most, cuts=(), kind=jnp.bfloat16):
    result = width * jax.random.normal(own_key, extent, jnp.float32)
    if cuts:
        result = result * shard_levels(own_key, extent, cuts, -0.22, 0.18)
    return jnp.clip(result, -most, most).astype(kind)


def setup_inputs(seed: int = 0) -> dict:
    splits = jax.random.split(jax.random.key(seed), 13)
    return {
        "cost": gaussian(splits[0], (DAYS, OPT, CLASSES), 1.0, 6.0, ((0, 32), (2, 8)), jnp.float32),
        "x_start": jnp.clip(1.0 * jax.random.uniform(splits[1], (DAYS, OPT, CLASSES), jnp.float32) ** shard_levels(splits[1], (DAYS, OPT, CLASSES), ((0, 32), (2, 8)), -0.2, 0.2), 0.0, 1.0),
        "ybal_start": gaussian(splits[2], (DAYS, CLASSES), 0.5, 3.0, ((0, 32), (1, 8)), jnp.float32),
        "inflow": jnp.clip(0.5 + 2.5 * jax.random.uniform(splits[3], (DAYS, CLASSES), jnp.float32) ** shard_levels(splits[3], (DAYS, CLASSES), ((0, 32), (1, 8)), -0.2, 0.2), 0.5, 3.0),
        "ycap_start": jnp.clip(-1.0 + 1.0 * jax.random.uniform(splits[4], (DAYS, FACILITIES), jnp.float32) ** shard_levels(splits[4], (DAYS, FACILITIES), ((0, 32), (1, 8)), -0.2, 0.2), -1.0, 0.0),
        "capacity": jnp.clip(jnp.exp(math.log(60.0) - 3.4011974 * jax.random.uniform(splits[5], (DAYS, FACILITIES), jnp.float32) ** shard_levels(splits[5], (DAYS, FACILITIES), ((0, 32), (1, 8)), -0.2, 0.2)), 2.0, 60.0),
        "upper": jnp.clip(jnp.exp(math.log(3.0) - 2.3025851 * jax.random.uniform(splits[6], (OPT, CLASSES), jnp.float32) ** shard_levels(splits[6], (OPT, CLASSES), ((1, 8),), -0.2, 0.2)), 0.3, 3.0),
        "facility": with_ends(skewed_ids(splits[7], (CLASSES,), FACILITIES, 2), jax.random.fold_in(splits[7], 3), 0, FACILITIES - 1).astype(jnp.int32),
        "option_count": with_ends(jax.random.randint(splits[8], (CLASSES,), 1, OPT + 1), jax.random.fold_in(splits[8], 1), 1, OPT).astype(jnp.int32),
        "decay_index": with_ends(jax.random.randint(splits[9], (CLASSES,), 0, LEVELS), jax.random.fold_in(splits[9], 1), 0, LEVELS - 1).astype(jnp.int32),
        "decay_table": jnp.clip(jax.random.uniform(splits[10], (LEVELS,), jnp.float32, 0.3, 0.99), 0.3, 0.99),
        "usage": jnp.clip(jnp.exp(jax.random.uniform(splits[11], (OPT,), jnp.float32, math.log(0.02), math.log(0.2))), 0.02, 0.2),
    }


ETA = 0.3

def balance(field, gamma):
    sums = lax.optimization_barrier(jnp.sum(field, axis=1))
    prior = jnp.concatenate([jnp.zeros((1, sums.shape[1]), jnp.float32), sums[:-1]], axis=0)
    return sums - gamma[None, :] * prior

def balance_t(duals, gamma):
    after = jnp.concatenate([duals[1:], jnp.zeros((1, duals.shape[1]), jnp.float32)], axis=0)
    return duals - gamma[None, :] * after

def capacity_use(field, usage, facility):
    weighted = lax.optimization_barrier(jnp.sum(usage[None, :, None] * field, axis=1))
    return jax.ops.segment_sum(weighted.T, facility, num_segments=FACILITIES).T

def reference(cost, x_start, ybal_start, inflow, ycap_start, capacity, upper, facility, option_count, decay_index, decay_table, usage):
    gamma = jnp.take(decay_table, decay_index)
    live = jnp.arange(OPT, dtype=jnp.int32)[:, None] < option_count[None, :]
    bound = jnp.where(live, upper, jnp.float32(0.0))
    field, duals, caps = (x_start, ybal_start, ycap_start)
    omega = jnp.float32(1.0)
    for step in range(ITERS):
        tau = ETA / omega
        sigma = ETA * omega
        pulled = jnp.take(caps, facility, axis=1)
        grad = cost - balance_t(duals, gamma)[:, None, :] - usage[None, :, None] * pulled[:, None, :]
        field_new = jnp.minimum(jnp.maximum(field - tau * grad, 0.0), bound[None])
        extra = 2.0 * field_new - field
        duals_new = duals - sigma * (balance(extra, gamma) - inflow)
        caps_new = jnp.minimum(caps - sigma * (capacity_use(extra, usage, facility) - capacity), 0.0)
        if step == 0:
            moved = jnp.sum((field_new - field) ** 2)
            dual_moved = jnp.sum((duals_new - duals) ** 2) + jnp.sum((caps_new - caps) ** 2)
            omega = jnp.sqrt(omega * jnp.sqrt((dual_moved + 1e-06) / (moved + 1e-06)))
        field, duals, caps = (field_new, duals_new, caps_new)
    return (field, duals, caps)
```

```python
import jax
import jax.numpy as jnp
from jax import lax
from jax.experimental import pallas as pl
from jax.experimental.pallas import tpu as pltpu
from jax.sharding import PartitionSpec as P

ETA = 0.3
EPS = 1e-6
LANES = 128
STEP = 256
PART = 1024
WIDE = 64

VM = pl.BlockSpec(memory_space=pltpu.VMEM)
SM = pl.BlockSpec(memory_space=pltpu.SMEM)
F32 = jnp.float32


def struct(*shape):
    return jax.ShapeDtypeStruct(shape, F32)


def call(body, name, outs, ins, scratch=(), cost=None):
    return pl.pallas_call(
        body,
        name=name,
        out_shape=outs,
        in_specs=ins,
        out_specs=[VM] * len(outs),
        scratch_shapes=list(scratch),
        compiler_params=pltpu.CompilerParams(vmem_limit_bytes=40 << 20),
        cost_estimate=cost,
    )


def rows_iota(shape):
    return lax.broadcasted_iota(jnp.int32, shape, 0)


def lanes_iota(shape):
    return lax.broadcasted_iota(jnp.int32, shape, 1)


def tile_of(ref, count, index):
    out = jnp.zeros(index.shape, F32)
    for k in range(count):
        out = jnp.where(index == k, ref[k], out)
    return out


def lookup(table, index):
    return jnp.take_along_axis(table, index, axis=1, mode="promise_in_bounds")


def folded(wide):
    out = wide[:, :LANES]
    for k in range(1, wide.shape[1] // LANES):
        out = out + wide[:, k * LANES : (k + 1) * LANES]
    return out


def pulled_of(caps, facility):
    days = caps.shape[0]
    parts = []
    for k in range(facility.shape[1] // LANES):
        own = jnp.broadcast_to(facility[:, k * LANES : (k + 1) * LANES], (days, LANES))
        low = jnp.bitwise_and(own, LANES - 1)
        got = lookup(caps[:, :LANES], low)
        for g in range(1, caps.shape[1] // LANES):
            got = jnp.where(own >= g * LANES, lookup(caps[:, g * LANES : (g + 1) * LANES], low), got)
        parts.append(got)
    return jnp.concatenate(parts, axis=1)


def gamma_of(table, index):
    parts = []
    for k in range(index.shape[1] // LANES):
        own = jnp.broadcast_to(index[:, k * LANES : (k + 1) * LANES], (8, LANES))
        parts.append(lookup(table, own))
    return jnp.concatenate(parts, axis=1)


def facility_sums(weighted_ref, facility_ref, facilities):
    days, classes = weighted_ref.shape
    groups = facilities // WIDE
    total = jnp.zeros((groups * 3 * days, WIDE), F32)
    for k in range(classes // PART):
        at = pl.ds(k * PART, PART)
        w = weighted_ref[:, at]
        fac = facility_ref[:, at]
        top = w.astype(jnp.bfloat16).astype(F32)
        rest = w - top
        mid = rest.astype(jnp.bfloat16).astype(F32)
        low = rest - mid
        group = jnp.broadcast_to(fac // WIDE, (days, PART))
        rows = []
        for g in range(groups):
            mine = group == g
            rows += [jnp.where(mine, top, 0.0), jnp.where(mine, mid, 0.0), jnp.where(mine, low, 0.0)]
        left = jnp.concatenate(rows, axis=0).astype(jnp.bfloat16)
        within = jnp.broadcast_to(jnp.bitwise_and(fac, WIDE - 1), (WIDE, PART))
        member = jnp.where(within == rows_iota((WIDE, PART)), 1.0, 0.0).astype(jnp.bfloat16)
        total = total + lax.dot_general(
            left, member, (((1,), (1,)), ((), ())), preferred_element_type=F32
        )
    out = []
    for g in range(groups):
        base = g * 3 * days
        out.append(
            total[base : base + days]
            + total[base + days : base + 2 * days]
            + total[base + 2 * days : base + 3 * days]
        )
    return out


def primal_rows(at, kt, pulled, tau, weights, bound, cost_ref, x_ref, x1_ref, sum_ref, weighted_ref, moved):
    for t in range(cost_ref.shape[0]):
        grad = cost_ref[t, :, at] - kt[t : t + 1] - weights * pulled[t : t + 1]
        old = x_ref[t, :, at]
        new = jnp.minimum(jnp.maximum(old - tau * grad, 0.0), bound)
        x1_ref[t, :, at] = new
        gone = new - old
        extra = new + gone
        sum_ref[t : t + 1, at] = jnp.sum(extra, axis=0, keepdims=True)
        weighted_ref[t : t + 1, at] = jnp.sum(weights * extra, axis=0, keepdims=True)
        if moved is not None:
            moved = moved + gone * gone
    return moved


def first_primal(
    usage_ref, table_ref, ends_ref, after_ref, cost_ref, x_ref, w_ref, inflow_ref, upper_ref,
    fac_ref, count_ref, index_ref,
    x1_ref, sum_ref, weighted_ref, last_ref, lead_ref, gamma_ref, moved_ref, caps_ref, room_ref,
):
    days, classes = w_ref.shape
    own = ends_ref.shape[2]
    for k in range(ends_ref.shape[0]):
        caps_ref[:, k * own : (k + 1) * own] = ends_ref[k, :days, :]
        room_ref[:, k * own : (k + 1) * own] = ends_ref[k, days:, :]
    caps = caps_ref[...]
    weights = tile_of(usage_ref, 8, rows_iota((8, STEP)))
    table = tile_of(table_ref, 16, lanes_iota((8, LANES)))
    rows = rows_iota((days, STEP))

    def step(j, moved):
        at = pl.ds(pl.multiple_of(j * STEP, STEP), STEP)
        gamma = gamma_of(table, index_ref[:, at])
        gamma_ref[:, at] = gamma[:1]
        bound = jnp.where(rows < count_ref[:, at], upper_ref[:, at], 0.0)
        w = w_ref[:, at]
        after = jnp.where(rows == days - 1, after_ref[:, at], pltpu.roll(w, days - 1, 0))
        moved = primal_rows(
            at, w - gamma * after, pulled_of(caps, fac_ref[:, at]), F32(ETA), weights, bound,
            cost_ref, x_ref, x1_ref, sum_ref, weighted_ref, moved,
        )
        last_ref[:, at] = sum_ref[days - 1 :, at]
        lead_ref[:, at] = w[:1] - ETA * (sum_ref[:1, at] - inflow_ref[:1, at])
        return moved

    moved = lax.fori_loop(0, classes // STEP, step, jnp.zeros((8, STEP), F32))
    moved_ref[...] = folded(moved)
    lead_ref[:, classes:] = jnp.ones((1, LANES), F32)


def first_use(weighted_ref, sum_ref, inflow_ref, gamma_ref, fac_ref, use_ref, moved_ref):
    days, classes = sum_ref.shape
    parts = facility_sums(weighted_ref, fac_ref, use_ref.shape[1])
    for g, part in enumerate(parts):
        use_ref[:, g * WIDE : (g + 1) * WIDE] = part
    total = jnp.zeros((days, PART), F32)
    for k in range(classes // PART):
        at = pl.ds(k * PART, PART)
        sums = sum_ref[:, at]
        gap = sums - gamma_ref[:, at] * pltpu.roll(sums, 1, 0) - inflow_ref[:, at]
        total = total + gap * gap
    moved_ref[...] = jnp.where(
        rows_iota((days, LANES)) > 0, (ETA * ETA) * folded(total), 0.0
    )


def first_send(use_ref, moved_ref, dual_ref, prior_ref, sum_ref, inflow_ref, gamma_ref, out_ref):
    days, classes = sum_ref.shape
    total = jnp.zeros((1, PART), F32)
    for k in range(classes // PART):
        at = pl.ds(k * PART, PART)
        gap = sum_ref[:1, at] - gamma_ref[:, at] * prior_ref[:, at] - inflow_ref[:1, at]
        total = total + gap * gap
    edge = (ETA * ETA) * folded(total)
    dual = dual_ref[...] + jnp.where(rows_iota((days, LANES)) == 0, edge, 0.0)
    use = use_ref[...]
    moved = moved_ref[...]
    for k in range(out_ref.shape[0]):
        out_ref[k, :days, :] = use
        out_ref[k, days:, :LANES] = moved
        out_ref[k, days:, LANES:] = dual


def caps_step(in_ref, caps_ref, room_ref, caps1_ref, out_ref):
    days = caps_ref.shape[0]
    total = in_ref[0]
    for k in range(1, in_ref.shape[0]):
        total = total + in_ref[k]
    caps = caps_ref[...]
    new = jnp.minimum(caps - ETA * (total[:days] - room_ref[...]), 0.0)
    caps1_ref[...] = new
    gone = new - caps
    primal = jnp.sum(total[days:, :LANES], axis=0, keepdims=True)
    dual = jnp.sum(total[days:, LANES:] + folded(gone * gone), axis=0, keepdims=True)
    rows = rows_iota((days, LANES))
    both = jnp.where(rows == 0, primal, jnp.where(rows == 1, dual, 0.0))
    for k in range(out_ref.shape[0]):
        out_ref[k] = both


def second_primal(
    usage_ref, moved_ref, caps_ref, cost_ref, x_ref, w_ref, inflow_ref, upper_ref, fac_ref, count_ref,
    gamma_ref, sums_ref, prior_ref, lead_ref,
    x2_ref, w1_ref, sum_ref, weighted_ref, last_ref, omega_ref,
):
    days, classes = w_ref.shape
    total = moved_ref[0]
    for k in range(1, moved_ref.shape[0]):
        total = total + moved_ref[k]
    primal = jnp.sum(total[0:1], axis=1, keepdims=True)
    dual = jnp.sum(total[1:2], axis=1, keepdims=True)
    omega = jnp.sqrt(jnp.sqrt((dual + EPS) / (primal + EPS)))
    omega_ref[...] = jnp.broadcast_to(omega, omega_ref.shape)
    tau = jnp.broadcast_to(ETA / omega, (8, STEP))
    caps = caps_ref[...]
    weights = tile_of(usage_ref, 8, rows_iota((8, STEP)))
    rows = rows_iota((days, STEP))
    more = ETA * jnp.max(lead_ref[:, classes:], axis=1, keepdims=True)

    def step(j, _):
        at = pl.ds(pl.multiple_of(j * STEP, STEP), STEP)
        gamma = gamma_ref[:, at]
        bound = jnp.where(rows < count_ref[:, at], upper_ref[:, at], 0.0)
        sums = sums_ref[:, at]
        prior = jnp.where(rows == 0, prior_ref[:, at], pltpu.roll(sums, 1, 0))
        w = w_ref[:, at] - ETA * (sums - gamma * prior - inflow_ref[:, at])
        w1_ref[:, at] = w
        edge = lead_ref[:, at] + more * gamma * sums[days - 1 :]
        after = jnp.where(rows == days - 1, edge, pltpu.roll(w, days - 1, 0))
        primal_rows(
            at, w - gamma * after, pulled_of(caps, fac_ref[:, at]), tau, weights, bound,
            cost_ref, x_ref, x2_ref, sum_ref, weighted_ref, None,
        )
        last_ref[:, at] = sum_ref[days - 1 :, at]
        return 0

    lax.fori_loop(0, classes // STEP, step, 0)


def second_use(weighted_ref, fac_ref, caps_ref, out_ref):
    days = weighted_ref.shape[0]
    parts = facility_sums(weighted_ref, fac_ref, caps_ref.shape[1])
    own = out_ref.shape[2]
    for k in range(out_ref.shape[0]):
        g, place = divmod(k * own, WIDE)
        out_ref[k, :days, :] = parts[g][:, place : place + own]
        out_ref[k, days:, :] = caps_ref[:, k * own : (k + 1) * own]


def last_duals(in_ref, room_ref, omega_ref, w_ref, sum_ref, prior_ref, inflow_ref, gamma_ref, w2_ref, caps2_ref):
    days, classes = w_ref.shape
    sigma = ETA * omega_ref[...]
    use = in_ref[0, :days]
    for k in range(1, in_ref.shape[0]):
        use = use + in_ref[k, :days]
    caps2_ref[...] = jnp.minimum(in_ref[0, days:] - sigma[:1, :1] * (use - room_ref[...]), 0.0)
    rows = rows_iota((days, LANES))
    for k in range(classes // LANES):
        at = pl.ds(k * LANES, LANES)
        sums = sum_ref[:, at]
        prior = jnp.where(rows == 0, prior_ref[:, at], pltpu.roll(sums, 1, 0))
        w2_ref[:, at] = w_ref[:, at] - sigma * (sums - gamma_ref[:, at] * prior - inflow_ref[:, at])


def to_next(row):
    n = lax.axis_size("day")
    return lax.ppermute(row, "day", [(i, i + 1) for i in range(n - 1)])


def to_previous(row):
    n = lax.axis_size("day")
    return lax.ppermute(row, "day", [(i + 1, i) for i in range(n - 1)])


def local(
    cost, x_start, ybal_start, inflow, ycap_start, capacity, upper, facility, option_count,
    decay_index, decay_table, usage,
):
    days, opts, classes = cost.shape
    own = ycap_start.shape[1]
    blocks = lax.axis_size("cls")
    facilities = own * blocks
    fac = facility.reshape(1, classes)
    count = option_count.reshape(1, classes)
    index = decay_index.reshape(1, classes)

    ends = jnp.broadcast_to(
        jnp.concatenate([ycap_start, capacity], axis=0)[None], (blocks, 2 * days, own)
    )
    after = to_previous(ybal_start[:1])
    ends = lax.all_to_all(ends, "cls", 0, 0)
    x1, sums, weighted, last, lead, gamma, moved, caps, room = call(
        first_primal, "first_primal",
        [struct(days, opts, classes), struct(days, classes), struct(days, classes), struct(1, classes),
         struct(1, classes + LANES), struct(1, classes), struct(8, LANES), struct(days, facilities),
         struct(days, facilities)],
        [SM, SM] + [VM] * 10,
    )(usage, decay_table, ends, after, cost, x_start, ybal_start, inflow, upper, fac, count, index)
    prior = to_next(last)
    lead = to_previous(lead)
    use, dual = call(
        first_use, "first_use", [struct(days, facilities), struct(days, LANES)], [VM] * 5,
        cost=pl.CostEstimate(flops=10_000_000, bytes_accessed=8_000_000, transcendentals=0),
    )(weighted, sums, inflow, gamma, fac)
    (sent,) = call(first_send, "first_send", [struct(blocks, 2 * days, facilities)], [VM] * 7)(
        use, moved, dual, prior, sums, inflow, gamma
    )
    got = lax.all_to_all(sent, "cls", 0, 0)
    caps1, sent = call(
        caps_step, "caps_step", [struct(days, facilities), struct(lax.axis_size("day"), days, LANES)],
        [VM] * 3,
    )(got, caps, room)
    got = lax.all_to_all(sent, "day", 0, 0)
    x2, w1, sums2, weighted2, last2, omega = call(
        second_primal, "second_primal",
        [struct(days, opts, classes), struct(days, classes), struct(days, classes), struct(days, classes),
         struct(1, classes), struct(8, LANES)],
        [SM] + [VM] * 13,
    )(usage, got, caps1, cost, x1, ybal_start, inflow, upper, fac, count, gamma, sums, prior, lead)
    prior2 = to_next(last2)
    (sent,) = call(
        second_use, "second_use", [struct(blocks, 2 * days, own)], [VM] * 3,
        cost=pl.CostEstimate(flops=10_000_000, bytes_accessed=8_000_000, transcendentals=0),
    )(weighted2, fac, caps1)
    got = lax.all_to_all(sent, "cls", 0, 0)
    w2, caps2 = call(last_duals, "last_duals", [struct(days, classes), struct(days, own)], [VM] * 8)(
        got, capacity, omega, w1, sums2, prior2, inflow, gamma
    )
    return x2, w2, caps2


def solution(mesh):
    in_specs = (
        P("day", None, "cls"), P("day", None, "cls"), P("day", "cls"), P("day", "cls"),
        P("day", "cls"), P("day", "cls"), P(None, "cls"), P("cls"), P("cls"), P("cls"), P(), P(),
    )
    out_specs = (P("day", None, "cls"), P("day", "cls"), P("day", "cls"))
    return jax.shard_map(local, mesh=mesh, in_specs=in_specs, out_specs=out_specs, check_vma=False)
```

```python
import jax
import jax.numpy as jnp
from jax import lax
from jax.experimental import pallas as pl
from jax.experimental.pallas import tpu as pltpu
from jax.sharding import PartitionSpec as P

ETA = 0.3
EPS = 1e-6
LANES = 128
BLOCK = 1024
STEP = 256
PART = 1024
WIDE = 64

VM = pl.BlockSpec(memory_space=pltpu.VMEM)
ANY = pl.BlockSpec(memory_space=pl.ANY)
F32 = jnp.float32


def struct(*shape):
    return jax.ShapeDtypeStruct(shape, F32)


def call(body, name, outs, ins, scratch=(), cost=None, limit=4, out_specs=None):
    return pl.pallas_call(
        body,
        name=name,
        out_shape=outs,
        in_specs=ins,
        out_specs=out_specs or [VM] * len(outs),
        scratch_shapes=list(scratch),
        compiler_params=pltpu.CompilerParams(vmem_limit_bytes=limit << 20),
        cost_estimate=cost,
    )


def in_hbm(*arrays):
    return [pltpu.with_memory_space_constraint(a, pltpu.HBM) for a in arrays]


def rows_iota(shape):
    return lax.broadcasted_iota(jnp.int32, shape, 0)


def lanes_iota(shape):
    return lax.broadcasted_iota(jnp.int32, shape, 1)


def tile_of(ref, count, index):
    out = jnp.zeros(index.shape, F32)
    for k in range(count):
        out = jnp.where(index == k, ref[k], out)
    return out


def lookup(table, index):
    return jnp.take_along_axis(table, index, axis=1, mode="promise_in_bounds")


def folded(wide):
    out = wide[:, :LANES]
    for k in range(1, wide.shape[1] // LANES):
        out = out + wide[:, k * LANES : (k + 1) * LANES]
    return out


def pulled_of(caps, facility):
    days = caps.shape[0]
    parts = []
    for k in range(facility.shape[1] // LANES):
        own = jnp.broadcast_to(facility[:, k * LANES : (k + 1) * LANES], (days, LANES))
        low = jnp.bitwise_and(own, LANES - 1)
        got = lookup(caps[:, :LANES], low)
        for g in range(1, caps.shape[1] // LANES):
            got = jnp.where(own >= g * LANES, lookup(caps[:, g * LANES : (g + 1) * LANES], low), got)
        parts.append(got)
    return jnp.concatenate(parts, axis=1)


def gamma_of(table, index):
    parts = []
    for k in range(index.shape[1] // LANES):
        own = jnp.broadcast_to(index[:, k * LANES : (k + 1) * LANES], (8, LANES))
        parts.append(lookup(table, own))
    return jnp.concatenate(parts, axis=1)


def facility_sums(weighted_ref, facility_ref, facilities):
    days, classes = weighted_ref.shape
    groups = facilities // WIDE
    total = jnp.zeros((groups * 3 * days, WIDE), F32)
    for k in range(classes // PART):
        at = pl.ds(k * PART, PART)
        w = weighted_ref[:, at]
        fac = facility_ref[:, at]
        top = w.astype(jnp.bfloat16).astype(F32)
        rest = w - top
        mid = rest.astype(jnp.bfloat16).astype(F32)
        low = rest - mid
        group = jnp.broadcast_to(fac // WIDE, (days, PART))
        rows = []
        for g in range(groups):
            mine = group == g
            rows += [jnp.where(mine, top, 0.0), jnp.where(mine, mid, 0.0), jnp.where(mine, low, 0.0)]
        left = jnp.concatenate(rows, axis=0).astype(jnp.bfloat16)
        within = jnp.broadcast_to(jnp.bitwise_and(fac, WIDE - 1), (WIDE, PART))
        member = jnp.where(within == rows_iota((WIDE, PART)), 1.0, 0.0).astype(jnp.bfloat16)
        total = total + lax.dot_general(
            left, member, (((1,), (1,)), ((), ())), preferred_element_type=F32
        )
    out = []
    for g in range(groups):
        base = g * 3 * days
        out.append(
            total[base : base + days]
            + total[base + days : base + 2 * days]
            + total[base + 2 * days : base + 3 * days]
        )
    return out


def primal_rows(at, kt, pulled, tau, weights, bound, cost_ref, x_ref, x1_ref, sum_ref, weighted_ref, moved):
    for t in range(cost_ref.shape[0]):
        grad = cost_ref[t, :, at] - kt[t : t + 1] - weights * pulled[t : t + 1]
        old = x_ref[t, :, at]
        new = jnp.minimum(jnp.maximum(old - tau * grad, 0.0), bound)
        x1_ref[t, :, at] = new
        gone = new - old
        extra = new + gone
        sum_ref[t : t + 1, at] = jnp.sum(extra, axis=0, keepdims=True)
        weighted_ref[t : t + 1, at] = jnp.sum(weights * extra, axis=0, keepdims=True)
        if moved is not None:
            moved = moved + gone * gone
    return moved


def start(caps_ref, room_ref, w_ref, out_ref, row_ref, caps, room, sems):
    copies = [
        pltpu.make_async_copy(caps_ref, caps, sems.at[0]),
        pltpu.make_async_copy(room_ref, room, sems.at[1]),
        pltpu.make_async_copy(w_ref.at[pl.ds(0, 1)], row_ref, sems.at[2]),
    ]
    for copy in copies:
        copy.start()
    out_ref[...] = jnp.zeros(out_ref.shape, F32)
    copies[0].wait()
    copies[1].wait()
    own = caps.shape[1]
    for k in range(out_ref.shape[0]):
        out_ref[k, :, :own] = caps[...]
        out_ref[k, :, own : 2 * own] = room[...]
    copies[2].wait()


def first_primal(
    usage_hbm, table_hbm, cost_hbm, x_hbm, w_hbm, inflow_hbm, upper_hbm, fac_hbm, count_hbm, index_hbm,
    ends_ref, after_ref,
    cost_ref, x1_ref, w_ref, inflow_ref, bound_ref, fac_ref,
    sum_ref, weighted_ref, last_ref, lead_ref, gamma_ref, moved_ref, caps_ref, room_ref, weights_ref,
    usage_ref, table_ref, count_ref, index_ref, sems,
):
    days, classes = w_ref.shape
    small = [
        (usage_hbm, usage_ref), (table_hbm, table_ref), (fac_hbm, fac_ref), (count_hbm, count_ref),
        (index_hbm, index_ref), (w_hbm, w_ref), (inflow_hbm, inflow_ref), (upper_hbm, bound_ref),
    ]
    small = [pltpu.make_async_copy(a, b, sems.at[k]) for k, (a, b) in enumerate(small)]
    large = []
    for k in range(classes // BLOCK):
        at = pl.ds(k * BLOCK, BLOCK)
        place = len(small) + 2 * k
        large.append((
            pltpu.make_async_copy(cost_hbm.at[:, :, at], cost_ref.at[:, :, at], sems.at[place]),
            pltpu.make_async_copy(x_hbm.at[:, :, at], x1_ref.at[:, :, at], sems.at[place + 1]),
        ))
    for copy in small:
        copy.start()
    for pair in large:
        for copy in pair:
            copy.start()
    own = caps_ref.shape[1] // ends_ref.shape[0]
    for k in range(ends_ref.shape[0]):
        caps_ref[:, k * own : (k + 1) * own] = ends_ref[k, :, :own]
        room_ref[:, k * own : (k + 1) * own] = ends_ref[k, :, own : 2 * own]
    caps = caps_ref[...]
    for copy in small:
        copy.wait()
    weights = tile_of(usage_ref, 8, rows_iota((8, LANES)))
    weights_ref[...] = weights
    weights = jnp.concatenate([weights] * (STEP // LANES), axis=1)
    table = tile_of(table_ref, 16, lanes_iota((8, LANES)))
    rows = rows_iota((days, STEP))

    def step(j, moved):
        at = pl.ds(pl.multiple_of(j * STEP, STEP), STEP)
        gamma = gamma_of(table, index_ref[:, at])
        gamma_ref[:, at] = gamma[:1]
        bound = jnp.where(rows < count_ref[:, at], bound_ref[:, at], 0.0)
        bound_ref[:, at] = bound
        w = w_ref[:, at]
        after = jnp.where(rows == days - 1, after_ref[:, at], pltpu.roll(w, days - 1, 0))
        moved = primal_rows(
            at, w - gamma * after, pulled_of(caps, fac_ref[:, at]), F32(ETA), weights, bound,
            cost_ref, x1_ref, x1_ref, sum_ref, weighted_ref, moved,
        )
        last_ref[:, at] = sum_ref[days - 1 :, at]
        lead_ref[:, at] = w[:1] - ETA * (sum_ref[:1, at] - inflow_ref[:1, at])
        return moved

    moved = jnp.zeros((8, STEP), F32)
    each = BLOCK // STEP
    for k, pair in enumerate(large):
        for copy in pair:
            copy.wait()
        moved = lax.fori_loop(k * each, (k + 1) * each, step, moved)
    moved_ref[...] = folded(moved)
    lead_ref[:, classes:] = jnp.ones((1, LANES), F32)


def first_use(weighted_ref, sum_ref, inflow_ref, gamma_ref, fac_ref, use_ref, moved_ref):
    days, classes = sum_ref.shape
    parts = facility_sums(weighted_ref, fac_ref, use_ref.shape[1])
    for g, part in enumerate(parts):
        use_ref[:, g * WIDE : (g + 1) * WIDE] = part
    total = jnp.zeros((days, PART), F32)
    for k in range(classes // PART):
        at = pl.ds(k * PART, PART)
        sums = sum_ref[:, at]
        gap = sums - gamma_ref[:, at] * pltpu.roll(sums, 1, 0) - inflow_ref[:, at]
        total = total + gap * gap
    moved_ref[...] = jnp.where(
        rows_iota((days, LANES)) > 0, (ETA * ETA) * folded(total), 0.0
    )


def first_send(use_ref, moved_ref, dual_ref, prior_ref, lead_ref, sum_ref, inflow_ref, gamma_ref, out_ref, edge_ref):
    days, classes = sum_ref.shape
    total = jnp.zeros((1, PART), F32)
    more = ETA * jnp.max(lead_ref[:, classes:], axis=1, keepdims=True)
    for k in range(classes // PART):
        at = pl.ds(k * PART, PART)
        edge_ref[:, at] = lead_ref[:, at] + more * (gamma_ref[:, at] * sum_ref[days - 1 :, at])
        gap = sum_ref[:1, at] - gamma_ref[:, at] * prior_ref[:, at] - inflow_ref[:1, at]
        total = total + gap * gap
    edge = (ETA * ETA) * folded(total)
    dual = dual_ref[...] + jnp.where(rows_iota((days, LANES)) == 0, edge, 0.0)
    use = use_ref[...]
    moved = moved_ref[...]
    for k in range(out_ref.shape[0]):
        out_ref[k, :days, :] = use
        out_ref[k, days:, :LANES] = moved
        out_ref[k, days:, LANES:] = dual


def caps_step(in_ref, caps_ref, room_ref, caps1_ref, out_ref):
    days = caps_ref.shape[0]
    total = in_ref[0]
    for k in range(1, in_ref.shape[0]):
        total = total + in_ref[k]
    caps = caps_ref[...]
    new = jnp.minimum(caps - ETA * (total[:days] - room_ref[...]), 0.0)
    caps1_ref[...] = new
    gone = new - caps
    primal = jnp.sum(total[days:, :LANES], axis=0, keepdims=True)
    dual = jnp.sum(total[days:, LANES:] + folded(gone * gone), axis=0, keepdims=True)
    rows = rows_iota((days, LANES))
    both = jnp.where(rows == 0, primal, jnp.where(rows == 1, dual, 0.0))
    for k in range(out_ref.shape[0]):
        out_ref[k] = both


def second_primal(
    moved_ref, weights_ref, caps_ref, cost_ref, x_ref, w_ref, inflow_ref, bound_ref, fac_ref,
    gamma_ref, sums_ref, prior_ref, edge_ref,
    out_hbm, w1_ref, sum_ref, weighted_ref, last_ref, omega_ref,
    x2_ref, sems,
):
    days, classes = w_ref.shape
    total = moved_ref[0]
    for k in range(1, moved_ref.shape[0]):
        total = total + moved_ref[k]
    primal = jnp.sum(total[0:1], axis=1, keepdims=True)
    dual = jnp.sum(total[1:2], axis=1, keepdims=True)
    omega = jnp.sqrt(jnp.sqrt((dual + EPS) / (primal + EPS)))
    omega_ref[...] = jnp.broadcast_to(omega, omega_ref.shape)
    tau = jnp.broadcast_to(ETA / omega, (8, STEP))
    caps = caps_ref[...]
    weights = jnp.concatenate([weights_ref[...]] * (STEP // LANES), axis=1)
    rows = rows_iota((days, STEP))

    def step(j, _):
        at = pl.ds(pl.multiple_of(j * STEP, STEP), STEP)
        gamma = gamma_ref[:, at]
        sums = sums_ref[:, at]
        prior = jnp.where(rows == 0, prior_ref[:, at], pltpu.roll(sums, 1, 0))
        w = w_ref[:, at] - ETA * (sums - gamma * prior - inflow_ref[:, at])
        w1_ref[:, at] = w
        after = jnp.where(rows == days - 1, edge_ref[:, at], pltpu.roll(w, days - 1, 0))
        primal_rows(
            at, w - gamma * after, pulled_of(caps, fac_ref[:, at]), tau, weights, bound_ref[:, at],
            cost_ref, x_ref, x2_ref, sum_ref, weighted_ref, None,
        )
        last_ref[:, at] = sum_ref[days - 1 :, at]
        return 0

    copies = []
    each = BLOCK // STEP
    for k in range(classes // BLOCK):
        lax.fori_loop(k * each, (k + 1) * each, step, 0)
        at = pl.ds(k * BLOCK, BLOCK)
        copies.append(pltpu.make_async_copy(x2_ref.at[:, :, at], out_hbm.at[:, :, at], sems.at[k]))
        copies[-1].start()
    for copy in copies:
        copy.wait()


def second_use(weighted_ref, fac_ref, caps_ref, out_ref):
    days = weighted_ref.shape[0]
    parts = facility_sums(weighted_ref, fac_ref, caps_ref.shape[1])
    own = caps_ref.shape[1] // out_ref.shape[0]
    out_ref[...] = jnp.zeros(out_ref.shape, F32)
    for k in range(out_ref.shape[0]):
        g, place = divmod(k * own, WIDE)
        out_ref[k, :, :own] = parts[g][:, place : place + own]
        out_ref[k, :, own : 2 * own] = caps_ref[:, k * own : (k + 1) * own]


def last_duals(in_ref, room_ref, omega_ref, w_ref, sum_ref, prior_ref, inflow_ref, gamma_ref, w2_ref, caps2_ref):
    days, classes = w_ref.shape
    sigma = ETA * omega_ref[...]
    own = room_ref.shape[1]
    use = in_ref[0, :, :own]
    for k in range(1, in_ref.shape[0]):
        use = use + in_ref[k, :, :own]
    caps2_ref[...] = jnp.minimum(
        in_ref[0, :, own : 2 * own] - sigma[:1, :1] * (use - room_ref[...]), 0.0
    )
    rows = rows_iota((days, LANES))
    for k in range(classes // LANES):
        at = pl.ds(k * LANES, LANES)
        sums = sum_ref[:, at]
        prior = jnp.where(rows == 0, prior_ref[:, at], pltpu.roll(sums, 1, 0))
        w2_ref[:, at] = w_ref[:, at] - sigma * (sums - gamma_ref[:, at] * prior - inflow_ref[:, at])


def to_next(row):
    n = lax.axis_size("day")
    return lax.ppermute(row, "day", [(i, i + 1) for i in range(n - 1)])


def to_previous(row):
    n = lax.axis_size("day")
    return lax.ppermute(row, "day", [(i + 1, i) for i in range(n - 1)])


def local(
    cost, x_start, ybal_start, inflow, ycap_start, capacity, upper, facility, option_count,
    decay_index, decay_table, usage,
):
    days, opts, classes = cost.shape
    own = ycap_start.shape[1]
    blocks = lax.axis_size("cls")
    facilities = own * blocks
    fac = facility.reshape(1, classes)
    count = option_count.reshape(1, classes)
    index = decay_index.reshape(1, classes)

    ends, row = call(
        start, "start", [struct(blocks, days, LANES), struct(1, classes)], [ANY] * 3,
        [pltpu.VMEM((days, own), F32), pltpu.VMEM((days, own), F32), pltpu.SemaphoreType.DMA((3,))],
    )(*in_hbm(ycap_start, capacity, ybal_start))
    after = to_previous(row)
    ends = lax.all_to_all(ends, "cls", 0, 0)
    (cost, x1, ybal_start, inflow, bound, fac, sums, weighted, last, lead, gamma, moved, caps, room,
     weights) = call(
        first_primal, "first_primal",
        [struct(days, opts, classes), struct(days, opts, classes), struct(days, classes),
         struct(days, classes), struct(opts, classes), jax.ShapeDtypeStruct((1, classes), jnp.int32),
         struct(days, classes), struct(days, classes), struct(1, classes),
         struct(1, classes + LANES), struct(1, classes), struct(8, LANES), struct(days, facilities),
         struct(days, facilities), struct(8, LANES)],
        [ANY] * 10 + [VM] * 2,
        [pltpu.SMEM((opts,), F32), pltpu.SMEM(decay_table.shape, F32), pltpu.VMEM((1, classes), jnp.int32),
         pltpu.VMEM((1, classes), jnp.int32), pltpu.SemaphoreType.DMA((8 + 2 * (classes // BLOCK),))],
    )(
        *in_hbm(usage, decay_table, cost, x_start, ybal_start, inflow, upper, fac, count, index), ends, after
    )
    prior = to_next(last)
    lead = to_previous(lead)
    use, dual = call(
        first_use, "first_use", [struct(days, facilities), struct(days, LANES)], [VM] * 5,
        cost=pl.CostEstimate(flops=10_000_000, bytes_accessed=8_000_000, transcendentals=0),
    )(weighted, sums, inflow, gamma, fac)
    sent, edge = call(
        first_send, "first_send", [struct(blocks, 2 * days, facilities), struct(1, classes)], [VM] * 8
    )(use, moved, dual, prior, lead, sums, inflow, gamma)
    got = lax.all_to_all(sent, "cls", 0, 0)
    caps1, sent = call(
        caps_step, "caps_step", [struct(days, facilities), struct(lax.axis_size("day"), days, LANES)],
        [VM] * 3,
    )(got, caps, room)
    got = lax.all_to_all(sent, "day", 0, 0)
    x2, w1, sums2, weighted2, last2, omega = call(
        second_primal, "second_primal",
        [struct(days, opts, classes), struct(days, classes), struct(days, classes), struct(days, classes),
         struct(1, classes), struct(8, LANES)],
        [VM] * 13,
        [pltpu.VMEM((days, opts, classes), F32), pltpu.SemaphoreType.DMA((classes // BLOCK,))],
        out_specs=[ANY] + [VM] * 5,
    )(got, weights, caps1, cost, x1, ybal_start, inflow, bound, fac, gamma, sums, prior, edge)
    prior2 = to_next(last2)
    (sent,) = call(
        second_use, "second_use", [struct(blocks, days, LANES)], [VM] * 3,
        cost=pl.CostEstimate(flops=10_000_000, bytes_accessed=8_000_000, transcendentals=0),
    )(weighted2, fac, caps1)
    got = lax.all_to_all(sent, "cls", 0, 0)
    w2, caps2 = call(last_duals, "last_duals", [struct(days, classes), struct(days, own)], [VM] * 8)(
        got, capacity, omega, w1, sums2, prior2, inflow, gamma
    )
    return x2, w2, caps2


def solution(mesh):
    in_specs = (
        P("day", None, "cls"), P("day", None, "cls"), P("day", "cls"), P("day", "cls"),
        P("day", "cls"), P("day", "cls"), P(None, "cls"), P("cls"), P("cls"), P("cls"), P(), P(),
    )
    out_specs = (P("day", None, "cls"), P("day", "cls"), P("day", "cls"))
    return jax.shard_map(local, mesh=mesh, in_specs=in_specs, out_specs=out_specs, check_vma=False)
```

```python
import jax
import jax.numpy as jnp
from jax import lax
from jax.experimental import pallas as pl
from jax.experimental.pallas import tpu as pltpu
from jax.sharding import PartitionSpec as P

ETA = 0.3
EPS = 1e-6
LANES = 128
STEP = 512
PART = 1024
BLOCK = 1024
WIDE = 64

VM = pl.BlockSpec(memory_space=pltpu.VMEM)
PASS = pl.CostEstimate(flops=10_000_000, bytes_accessed=8_000_000, transcendentals=0)
ANY = pl.BlockSpec(memory_space=pl.ANY)
F32 = jnp.float32


def struct(*shape):
    return jax.ShapeDtypeStruct(shape, F32)


def call(body, name, outs, ins, scratch=(), cost=None, limit=4, out_specs=None):
    return pl.pallas_call(
        body,
        name=name,
        out_shape=outs,
        in_specs=ins,
        out_specs=out_specs or [VM] * len(outs),
        scratch_shapes=list(scratch),
        compiler_params=pltpu.CompilerParams(vmem_limit_bytes=limit << 20),
        cost_estimate=cost,
    )


def in_hbm(*arrays):
    return [pltpu.with_memory_space_constraint(a, pltpu.HBM) for a in arrays]


def rows_iota(shape):
    return lax.broadcasted_iota(jnp.int32, shape, 0)


def lanes_iota(shape):
    return lax.broadcasted_iota(jnp.int32, shape, 1)


def tile_of(ref, count, index):
    out = jnp.zeros(index.shape, F32)
    for k in range(count):
        out = jnp.where(index == k, ref[k], out)
    return out


def lookup(table, index):
    return jnp.take_along_axis(table, index, axis=1, mode="promise_in_bounds")


def folded(wide):
    out = wide[:, :LANES]
    for k in range(1, wide.shape[1] // LANES):
        out = out + wide[:, k * LANES : (k + 1) * LANES]
    return out


def pulled_of(caps, facility):
    days = caps.shape[0]
    parts = []
    for k in range(facility.shape[1] // LANES):
        own = jnp.broadcast_to(facility[:, k * LANES : (k + 1) * LANES], (days, LANES))
        low = jnp.bitwise_and(own, LANES - 1)
        got = lookup(caps[:, :LANES], low)
        for g in range(1, caps.shape[1] // LANES):
            got = jnp.where(own >= g * LANES, lookup(caps[:, g * LANES : (g + 1) * LANES], low), got)
        parts.append(got)
    return jnp.concatenate(parts, axis=1)


def gamma_of(table, index):
    parts = []
    for k in range(index.shape[1] // LANES):
        own = jnp.broadcast_to(index[:, k * LANES : (k + 1) * LANES], (8, LANES))
        parts.append(lookup(table, own))
    return jnp.concatenate(parts, axis=1)


def facility_sums(weighted_ref, facility_ref, facilities):
    days, classes = weighted_ref.shape
    groups = facilities // WIDE
    total = jnp.zeros((groups * 3 * days, WIDE), F32)
    for k in range(classes // PART):
        at = pl.ds(k * PART, PART)
        w = weighted_ref[:, at]
        fac = facility_ref[:, at]
        top = w.astype(jnp.bfloat16).astype(F32)
        rest = w - top
        mid = rest.astype(jnp.bfloat16).astype(F32)
        low = rest - mid
        group = jnp.broadcast_to(fac // WIDE, (days, PART))
        rows = []
        for g in range(groups):
            mine = group == g
            rows += [jnp.where(mine, top, 0.0), jnp.where(mine, mid, 0.0), jnp.where(mine, low, 0.0)]
        left = jnp.concatenate(rows, axis=0).astype(jnp.bfloat16)
        within = jnp.broadcast_to(jnp.bitwise_and(fac, WIDE - 1), (WIDE, PART))
        member = jnp.where(within == rows_iota((WIDE, PART)), 1.0, 0.0).astype(jnp.bfloat16)
        total = total + lax.dot_general(
            left, member, (((1,), (1,)), ((), ())), preferred_element_type=F32
        )
    out = []
    for g in range(groups):
        base = g * 3 * days
        out.append(
            total[base : base + days]
            + total[base + days : base + 2 * days]
            + total[base + 2 * days : base + 3 * days]
        )
    return out


def combined(a, b, mask, distance):
    return jnp.where(mask, a, b) + pltpu.roll(jnp.where(mask, b, a), distance, 0)


def row_sums(tiles):
    rows = rows_iota(tiles[0].shape)
    for distance in (1, 2, 4):
        mask = jnp.bitwise_and(rows, distance) == 0
        tiles = [combined(tiles[k], tiles[k + 1], mask, distance) for k in range(0, len(tiles), 2)]
    return tiles[0]


def spread(tile, row):
    return jnp.broadcast_to(tile[row : row + 1], tile.shape)


def start(caps_ref, room_ref, w_ref, out_ref, row_ref, caps, room, sems):
    copies = [
        pltpu.make_async_copy(caps_ref, caps, sems.at[0]),
        pltpu.make_async_copy(room_ref, room, sems.at[1]),
        pltpu.make_async_copy(w_ref.at[pl.ds(0, 1)], row_ref, sems.at[2]),
    ]
    for copy in copies:
        copy.start()
    out_ref[...] = jnp.zeros(out_ref.shape, F32)
    copies[0].wait()
    copies[1].wait()
    own = caps.shape[1]
    for k in range(out_ref.shape[0]):
        out_ref[k, :, :own] = caps[...]
        out_ref[k, :, own : 2 * own] = room[...]
    copies[2].wait()


def lanes_of(j, u):
    return pl.ds(pl.multiple_of(j * STEP, STEP) + u * LANES, LANES)


def block_copies(pairs, sems):
    classes = pairs[0][0].shape[2]
    return [
        [
            pltpu.make_async_copy(
                a.at[:, :, pl.ds(k * BLOCK, BLOCK)], b.at[:, :, pl.ds(k * BLOCK, BLOCK)], sems.at[n, k]
            )
            for n, (a, b) in enumerate(pairs)
        ]
        for k in range(classes // BLOCK)
    ]


def start_all(blocks):
    for block in blocks:
        for copy in block:
            copy.start()


def wait_all(block):
    for copy in block:
        copy.wait()


def load(
    usage_hbm, table_hbm, w_hbm, inflow_hbm, upper_hbm, fac_hbm, count_hbm, index_hbm,
    kt_ref, w_ref, inflow_ref, bound_ref, fac_ref, gamma_ref, weights_ref,
    usage_ref, table_ref, count_ref, index_ref, sems,
):
    days, classes = w_ref.shape
    small = [
        (usage_hbm, usage_ref), (table_hbm, table_ref), (fac_hbm, fac_ref), (count_hbm, count_ref),
        (index_hbm, index_ref), (w_hbm, w_ref), (inflow_hbm, inflow_ref), (upper_hbm, bound_ref),
    ]
    small = [pltpu.make_async_copy(a, b, sems.at[k]) for k, (a, b) in enumerate(small)]
    for copy in small:
        copy.start()
    for copy in small:
        copy.wait()
    weights_ref[...] = tile_of(usage_ref, 8, rows_iota((8, LANES)))
    table = tile_of(table_ref, 16, lanes_iota((8, LANES)))
    rows = rows_iota((days, LANES))

    def step(j, _):
        for u in range(STEP // LANES):
            at = lanes_of(j, u)
            gamma = gamma_of(table, index_ref[:, at])
            gamma_ref[:, at] = gamma[:1]
            bound_ref[:, at] = jnp.where(rows < count_ref[:, at], bound_ref[:, at], 0.0)
            w = w_ref[:, at]
            kt_ref[:, at] = w - gamma * jnp.where(rows == days - 1, 0.0, pltpu.roll(w, days - 1, 0))
        return 0

    lax.fori_loop(0, classes // STEP, step, 0)


def first_primal(
    cost_hbm, x_hbm, weights_ref, ends_ref, after_ref, kt_ref, w_ref, inflow_ref, bound_ref, fac_ref, gamma_ref,
    x1_hbm, sum_ref, weighted_ref, last_ref, lead_ref, moved_ref, caps_ref, room_ref,
    cost_ref, x_ref, sems,
):
    days, classes = w_ref.shape
    arrive = block_copies([(cost_hbm, cost_ref), (x_hbm, x_ref)], sems)
    leave = block_copies([(x_ref, x1_hbm)], sems.at[2:])
    start_all(arrive)
    own = caps_ref.shape[1] // ends_ref.shape[0]
    for k in range(ends_ref.shape[0]):
        caps_ref[:, k * own : (k + 1) * own] = ends_ref[k, :, :own]
        room_ref[:, k * own : (k + 1) * own] = ends_ref[k, :, own : 2 * own]
    caps = caps_ref[...]
    weights = weights_ref[...]
    rows = rows_iota((days, LANES))

    def step(j, moved):
        moved = list(moved)
        for u in range(STEP // LANES):
            at = lanes_of(j, u)
            bound = bound_ref[:, at]
            pulled = pulled_of(caps, fac_ref[:, at])
            kt = kt_ref[:, at]
            kt = jnp.where(rows == days - 1, kt - gamma_ref[:, at] * after_ref[:, at], kt)
            sums, weighted = [], []
            for t in range(days):
                old = x_ref[t, :, at]
                grad = cost_ref[t, :, at] - spread(kt, t) - weights * spread(pulled, t)
                new = jnp.minimum(jnp.maximum(old - ETA * grad, 0.0), bound)
                x_ref[t, :, at] = new
                gone = new - old
                moved[u] = moved[u] + gone * gone
                extra = new + gone
                sums.append(extra)
                weighted.append(weights * extra)
            sums = row_sums(sums)
            sum_ref[:, at] = sums
            weighted_ref[:, at] = row_sums(weighted)
            last_ref[:, at] = sums[days - 1 :]
            lead_ref[:, at] = w_ref[:1, at] - ETA * (sums[:1] - inflow_ref[:1, at])
        return tuple(moved)

    zero = jnp.zeros((8, LANES), F32)
    moved = (zero,) * (STEP // LANES)
    each = BLOCK // STEP
    for k, block in enumerate(arrive):
        wait_all(block)
        moved = lax.fori_loop(k * each, (k + 1) * each, step, moved)
        start_all(leave[k : k + 1])
    total = moved[0]
    for part in moved[1:]:
        total = total + part
    moved_ref[...] = total
    lead_ref[:, classes:] = jnp.ones((1, LANES), F32)
    for block in leave:
        wait_all(block)


def first_use(weighted_ref, sum_ref, inflow_ref, gamma_ref, fac_ref, use_ref, moved_ref):
    days, classes = sum_ref.shape
    parts = facility_sums(weighted_ref, fac_ref, use_ref.shape[1])
    for g, part in enumerate(parts):
        use_ref[:, g * WIDE : (g + 1) * WIDE] = part
    total = jnp.zeros((days, PART), F32)
    for k in range(classes // PART):
        at = pl.ds(k * PART, PART)
        sums = sum_ref[:, at]
        gap = sums - gamma_ref[:, at] * pltpu.roll(sums, 1, 0) - inflow_ref[:, at]
        total = total + gap * gap
    moved_ref[...] = jnp.where(
        rows_iota((days, LANES)) > 0, (ETA * ETA) * folded(total), 0.0
    )


def first_send(use_ref, moved_ref, dual_ref, prior_ref, sum_ref, inflow_ref, gamma_ref, out_ref):
    days, classes = sum_ref.shape
    total = jnp.zeros((1, PART), F32)
    for k in range(classes // PART):
        at = pl.ds(k * PART, PART)
        gap = sum_ref[:1, at] - gamma_ref[:, at] * prior_ref[:, at] - inflow_ref[:1, at]
        total = total + gap * gap
    edge = (ETA * ETA) * folded(total)
    dual = dual_ref[...] + jnp.where(rows_iota((days, LANES)) == 0, edge, 0.0)
    use = use_ref[...]
    moved = moved_ref[...]
    for k in range(out_ref.shape[0]):
        out_ref[k, :days, :] = use
        out_ref[k, days:, :LANES] = moved
        out_ref[k, days:, LANES:] = dual


def caps_step(in_ref, caps_ref, room_ref, caps1_ref, out_ref):
    days = caps_ref.shape[0]
    total = in_ref[0]
    for k in range(1, in_ref.shape[0]):
        total = total + in_ref[k]
    caps = caps_ref[...]
    new = jnp.minimum(caps - ETA * (total[:days] - room_ref[...]), 0.0)
    caps1_ref[...] = new
    gone = new - caps
    primal = jnp.sum(total[days:, :LANES], axis=0, keepdims=True)
    dual = jnp.sum(total[days:, LANES:] + folded(gone * gone), axis=0, keepdims=True)
    rows = rows_iota((days, LANES))
    both = jnp.where(rows == 0, primal, jnp.where(rows == 1, dual, 0.0))
    for k in range(out_ref.shape[0]):
        out_ref[k] = both


def next_duals(
    w_ref, sum_ref, inflow_ref, gamma_ref, prior_ref, lead_ref, caps_ref, w1_ref, kt_ref, caps_out_ref
):
    days, classes = w_ref.shape
    rows = rows_iota((days, LANES))
    more = ETA * lead_ref[:, classes:]
    caps_out_ref[...] = caps_ref[...]
    for k in range(classes // LANES):
        at = pl.ds(k * LANES, LANES)
        gamma = gamma_ref[:, at]
        sums = sum_ref[:, at]
        prior = jnp.where(rows == 0, prior_ref[:, at], pltpu.roll(sums, 1, 0))
        w = w_ref[:, at] - ETA * (sums - gamma * prior - inflow_ref[:, at])
        w1_ref[:, at] = w
        edge = lead_ref[:, at] + more * (gamma * sums[days - 1 :])
        kt_ref[:, at] = w - gamma * jnp.where(rows == days - 1, edge, pltpu.roll(w, days - 1, 0))


def next_grad(cost_hbm, weights_ref, caps_ref, kt_ref, fac_ref, grad_ref, sems):
    days, classes = kt_ref.shape
    arrive = block_copies([(cost_hbm, grad_ref)], sems)
    start_all(arrive)
    caps = caps_ref[...]
    weights = weights_ref[...]

    def step(j, _):
        for u in range(STEP // LANES):
            at = lanes_of(j, u)
            pulled = pulled_of(caps, fac_ref[:, at])
            kt = kt_ref[:, at]
            for t in range(days):
                grad_ref[t, :, at] = grad_ref[t, :, at] - spread(kt, t) - weights * spread(pulled, t)
        return 0

    each = BLOCK // STEP
    for k, block in enumerate(arrive):
        wait_all(block)
        lax.fori_loop(k * each, (k + 1) * each, step, 0)


def second_primal(
    x_hbm, moved_ref, weights_ref, grad_ref, bound_ref,
    x2_hbm, sum_ref, weighted_ref, last_ref, omega_ref,
    x_ref, sems,
):
    days, classes = sum_ref.shape
    arrive = block_copies([(x_hbm, x_ref)], sems)
    leave = block_copies([(x_ref, x2_hbm)], sems.at[1:])
    start_all(arrive)
    total = moved_ref[0]
    for k in range(1, moved_ref.shape[0]):
        total = total + moved_ref[k]
    primal = jnp.sum(total[0:1], axis=1, keepdims=True)
    dual = jnp.sum(total[1:2], axis=1, keepdims=True)
    omega = jnp.sqrt(jnp.sqrt((dual + EPS) / (primal + EPS)))
    omega_ref[...] = jnp.broadcast_to(omega, omega_ref.shape)
    tau = jnp.broadcast_to(ETA / omega, (8, LANES))
    weights = weights_ref[...]

    def step(j, _):
        for u in range(STEP // LANES):
            at = lanes_of(j, u)
            bound = bound_ref[:, at]
            sums, weighted = [], []
            for t in range(days):
                old = x_ref[t, :, at]
                new = jnp.minimum(jnp.maximum(old - tau * grad_ref[t, :, at], 0.0), bound)
                x_ref[t, :, at] = new
                extra = new + (new - old)
                sums.append(extra)
                weighted.append(weights * extra)
            sums = row_sums(sums)
            sum_ref[:, at] = sums
            weighted_ref[:, at] = row_sums(weighted)
            last_ref[:, at] = sums[days - 1 :]
        return 0

    each = BLOCK // STEP
    for k, block in enumerate(arrive):
        wait_all(block)
        lax.fori_loop(k * each, (k + 1) * each, step, 0)
        start_all(leave[k : k + 1])
    for block in leave:
        wait_all(block)


def second_use(weighted_ref, fac_ref, caps_ref, out_ref):
    days = weighted_ref.shape[0]
    parts = facility_sums(weighted_ref, fac_ref, caps_ref.shape[1])
    own = caps_ref.shape[1] // out_ref.shape[0]
    out_ref[...] = jnp.zeros(out_ref.shape, F32)
    for k in range(out_ref.shape[0]):
        g, place = divmod(k * own, WIDE)
        out_ref[k, :, :own] = parts[g][:, place : place + own]
        out_ref[k, :, own : 2 * own] = caps_ref[:, k * own : (k + 1) * own]


def last_duals(in_ref, room_ref, omega_ref, w_ref, sum_ref, prior_ref, inflow_ref, gamma_ref, w2_ref, caps2_ref):
    days, classes = w_ref.shape
    sigma = ETA * omega_ref[...]
    own = room_ref.shape[1]
    use = in_ref[0, :, :own]
    for k in range(1, in_ref.shape[0]):
        use = use + in_ref[k, :, :own]
    caps2_ref[...] = jnp.minimum(
        in_ref[0, :, own : 2 * own] - sigma[:1, :1] * (use - room_ref[...]), 0.0
    )
    rows = rows_iota((days, LANES))
    for k in range(classes // LANES):
        at = pl.ds(k * LANES, LANES)
        sums = sum_ref[:, at]
        prior = jnp.where(rows == 0, prior_ref[:, at], pltpu.roll(sums, 1, 0))
        w2_ref[:, at] = w_ref[:, at] - sigma * (sums - gamma_ref[:, at] * prior - inflow_ref[:, at])


def to_next(row):
    n = lax.axis_size("day")
    return lax.ppermute(row, "day", [(i, i + 1) for i in range(n - 1)])


def to_previous(row):
    n = lax.axis_size("day")
    return lax.ppermute(row, "day", [(i + 1, i) for i in range(n - 1)])


def local(
    cost, x_start, ybal_start, inflow, ycap_start, capacity, upper, facility, option_count,
    decay_index, decay_table, usage,
):
    days, opts, classes = cost.shape
    own = ycap_start.shape[1]
    blocks = lax.axis_size("cls")
    facilities = own * blocks
    fac = facility.reshape(1, classes)
    count = option_count.reshape(1, classes)
    index = decay_index.reshape(1, classes)

    ends, row = call(
        start, "start", [struct(blocks, days, LANES), struct(1, classes)], [ANY] * 3,
        [pltpu.VMEM((days, own), F32), pltpu.VMEM((days, own), F32), pltpu.SemaphoreType.DMA((3,))],
    )(*in_hbm(ycap_start, capacity, ybal_start))
    after = to_previous(row)
    ends = lax.all_to_all(ends, "cls", 0, 0)
    field, rows, row, tile = (
        struct(days, opts, classes), struct(days, classes), struct(1, classes), struct(8, LANES)
    )
    table = struct(days, facilities)
    kt, w, inflow, bound, fac, gamma, weights = call(
        load, "load",
        [rows, rows, rows, struct(opts, classes),
         jax.ShapeDtypeStruct((1, classes), jnp.int32), row, tile],
        [ANY] * 8,
        [pltpu.SMEM((opts,), F32), pltpu.SMEM(decay_table.shape, F32), pltpu.VMEM((1, classes), jnp.int32),
         pltpu.VMEM((1, classes), jnp.int32), pltpu.SemaphoreType.DMA((8,))],
        cost=PASS,
    )(*in_hbm(usage, decay_table, ybal_start, inflow, upper, fac, count, index))
    streams = classes // BLOCK
    x1, sums, weighted, last, lead, moved, caps, room = call(
        first_primal, "first_primal",
        [pltpu.HBM(field.shape, F32), rows, rows, row, struct(1, classes + LANES), tile, table, table],
        [ANY] * 2 + [VM] * 9,
        [pltpu.VMEM(field.shape, F32), pltpu.VMEM(field.shape, F32), pltpu.SemaphoreType.DMA((3, streams))],
        limit=8, out_specs=[ANY] + [VM] * 7,
    )(*in_hbm(cost, x_start), weights, ends, after, kt, w, inflow, bound, fac, gamma)
    prior = to_next(last)
    lead = to_previous(lead)
    use, dual = call(
        first_use, "first_use", [struct(days, facilities), struct(days, LANES)], [VM] * 5,
        cost=PASS,
    )(weighted, sums, inflow, gamma, fac)
    (sent,) = call(first_send, "first_send", [struct(blocks, 2 * days, facilities)], [VM] * 7)(
        use, moved, dual, prior, sums, inflow, gamma
    )
    got = lax.all_to_all(sent, "cls", 0, 0)
    w1, kt, caps = call(next_duals, "next_duals", [rows, rows, table], [VM] * 7, cost=PASS)(
        w, sums, inflow, gamma, prior, lead, caps
    )
    caps1, sent = call(
        caps_step, "caps_step", [table, struct(lax.axis_size("day"), days, LANES)], [VM] * 3
    )(got, caps, room)
    got = lax.all_to_all(sent, "day", 0, 0)
    (grad,) = call(
        next_grad, "next_grad", [field], [ANY] + [VM] * 4, [pltpu.SemaphoreType.DMA((1, streams))], cost=PASS
    )(*in_hbm(cost), weights, caps1, kt, fac)
    x2, sums2, weighted2, last2, omega = call(
        second_primal, "second_primal", [pltpu.HBM(field.shape, F32), rows, rows, row, tile],
        [ANY] + [VM] * 4, [pltpu.VMEM(field.shape, F32), pltpu.SemaphoreType.DMA((2, streams))],
        limit=8, out_specs=[ANY] + [VM] * 4,
    )(*in_hbm(x1), got, weights, grad, bound)
    prior2 = to_next(last2)
    (sent,) = call(
        second_use, "second_use", [struct(blocks, days, LANES)], [VM] * 3,
        cost=PASS,
    )(weighted2, fac, caps1)
    got = lax.all_to_all(sent, "cls", 0, 0)
    w2, caps2 = call(last_duals, "last_duals", [struct(days, classes), struct(days, own)], [VM] * 8)(
        got, capacity, omega, w1, sums2, prior2, inflow, gamma
    )
    return x2, w2, caps2


def solution(mesh):
    in_specs = (
        P("day", None, "cls"), P("day", None, "cls"), P("day", "cls"), P("day", "cls"),
        P("day", "cls"), P("day", "cls"), P(None, "cls"), P("cls"), P("cls"), P("cls"), P(), P(),
    )
    out_specs = (P("day", None, "cls"), P("day", "cls"), P("day", "cls"))
    return jax.shard_map(local, mesh=mesh, in_specs=in_specs, out_specs=out_specs, check_vma=False)
```

```python
import jax
import jax.numpy as jnp
from jax import lax
from jax.experimental import pallas as pl
from jax.experimental.pallas import tpu as pltpu
from jax.sharding import PartitionSpec as P

ETA = 0.3
EPS = 1e-6
LANES = 128
STEP = 512
PART = 1024
BLOCK = 1024
WIDE = 64

VM = pl.BlockSpec(memory_space=pltpu.VMEM)
PASS = pl.CostEstimate(flops=10_000_000, bytes_accessed=8_000_000, transcendentals=0)
ANY = pl.BlockSpec(memory_space=pl.ANY)
F32 = jnp.float32


def struct(*shape):
    return jax.ShapeDtypeStruct(shape, F32)


def call(body, name, outs, ins, scratch=(), cost=None, limit=4, out_specs=None):
    return pl.pallas_call(
        body,
        name=name,
        out_shape=outs,
        in_specs=ins,
        out_specs=out_specs or [VM] * len(outs),
        scratch_shapes=list(scratch),
        compiler_params=pltpu.CompilerParams(vmem_limit_bytes=limit << 20),
        cost_estimate=cost,
    )


def in_hbm(*arrays):
    return [pltpu.with_memory_space_constraint(a, pltpu.HBM) for a in arrays]


def rows_iota(shape):
    return lax.broadcasted_iota(jnp.int32, shape, 0)


def lanes_iota(shape):
    return lax.broadcasted_iota(jnp.int32, shape, 1)


def tile_of(ref, count, index):
    out = jnp.zeros(index.shape, F32)
    for k in range(count):
        out = jnp.where(index == k, ref[k], out)
    return out


def lookup(table, index):
    return jnp.take_along_axis(table, index, axis=1, mode="promise_in_bounds")


def folded(wide):
    out = wide[:, :LANES]
    for k in range(1, wide.shape[1] // LANES):
        out = out + wide[:, k * LANES : (k + 1) * LANES]
    return out


def pulled_of(caps, facility):
    days = caps.shape[0]
    parts = []
    for k in range(facility.shape[1] // LANES):
        own = jnp.broadcast_to(facility[:, k * LANES : (k + 1) * LANES], (days, LANES))
        low = jnp.bitwise_and(own, LANES - 1)
        got = lookup(caps[:, :LANES], low)
        for g in range(1, caps.shape[1] // LANES):
            got = jnp.where(own >= g * LANES, lookup(caps[:, g * LANES : (g + 1) * LANES], low), got)
        parts.append(got)
    return jnp.concatenate(parts, axis=1)


def gamma_of(table, index):
    parts = []
    for k in range(index.shape[1] // LANES):
        own = jnp.broadcast_to(index[:, k * LANES : (k + 1) * LANES], (8, LANES))
        parts.append(lookup(table, own))
    return jnp.concatenate(parts, axis=1)


def facility_part(weighted, facility, groups):
    days, classes = weighted.shape
    top = weighted.astype(jnp.bfloat16).astype(F32)
    rest = weighted - top
    mid = rest.astype(jnp.bfloat16).astype(F32)
    low = rest - mid
    group = jnp.broadcast_to(facility // WIDE, (days, classes))
    rows = []
    for g in range(groups):
        mine = group == g
        rows += [jnp.where(mine, top, 0.0), jnp.where(mine, mid, 0.0), jnp.where(mine, low, 0.0)]
    left = jnp.concatenate(rows, axis=0).astype(jnp.bfloat16)
    within = jnp.broadcast_to(jnp.bitwise_and(facility, WIDE - 1), (WIDE, classes))
    member = jnp.where(within == rows_iota((WIDE, classes)), 1.0, 0.0).astype(jnp.bfloat16)
    return lax.dot_general(left, member, (((1,), (1,)), ((), ())), preferred_element_type=F32)


def facility_groups(total, days):
    parts = [total[k : k + days] for k in range(0, total.shape[0], days)]
    return [parts[k] + parts[k + 1] + parts[k + 2] for k in range(0, len(parts), 3)]


def combined(a, b, mask, distance):
    return jnp.where(mask, a, b) + pltpu.roll(jnp.where(mask, b, a), distance, 0)


def row_sums(tiles):
    rows = rows_iota(tiles[0].shape)
    for distance in (1, 2, 4):
        mask = jnp.bitwise_and(rows, distance) == 0
        tiles = [combined(tiles[k], tiles[k + 1], mask, distance) for k in range(0, len(tiles), 2)]
    return tiles[0]


def spread(tile, row):
    return jnp.broadcast_to(tile[row : row + 1], tile.shape)


def start(caps_ref, room_ref, w_ref, out_ref, row_ref, caps, room, sems):
    copies = [
        pltpu.make_async_copy(caps_ref, caps, sems.at[0]),
        pltpu.make_async_copy(room_ref, room, sems.at[1]),
        pltpu.make_async_copy(w_ref.at[pl.ds(0, 1)], row_ref, sems.at[2]),
    ]
    for copy in copies:
        copy.start()
    out_ref[...] = jnp.zeros(out_ref.shape, F32)
    copies[0].wait()
    copies[1].wait()
    own = caps.shape[1]
    for k in range(out_ref.shape[0]):
        out_ref[k, :, :own] = caps[...]
        out_ref[k, :, own : 2 * own] = room[...]
    copies[2].wait()


def lanes_of(j, u):
    return pl.ds(pl.multiple_of(j * STEP, STEP) + u * LANES, LANES)


def block_copies(pairs, sems):
    classes = pairs[0][0].shape[2]
    return [
        [
            pltpu.make_async_copy(
                a.at[:, :, pl.ds(k * BLOCK, BLOCK)], b.at[:, :, pl.ds(k * BLOCK, BLOCK)], sems.at[n, k]
            )
            for n, (a, b) in enumerate(pairs)
        ]
        for k in range(classes // BLOCK)
    ]


def start_all(blocks):
    for block in blocks:
        for copy in block:
            copy.start()


def wait_all(block):
    for copy in block:
        copy.wait()


def load(
    usage_hbm, table_hbm, w_hbm, inflow_hbm, upper_hbm, fac_hbm, count_hbm, index_hbm,
    kt_ref, w_ref, inflow_ref, bound_ref, fac_ref, gamma_ref, weights_ref,
    usage_ref, table_ref, count_ref, index_ref, sems,
):
    days, classes = w_ref.shape
    small = [
        (usage_hbm, usage_ref), (table_hbm, table_ref), (fac_hbm, fac_ref), (count_hbm, count_ref),
        (index_hbm, index_ref), (w_hbm, w_ref), (inflow_hbm, inflow_ref), (upper_hbm, bound_ref),
    ]
    small = [pltpu.make_async_copy(a, b, sems.at[k]) for k, (a, b) in enumerate(small)]
    for copy in small:
        copy.start()
    for copy in small:
        copy.wait()
    weights_ref[...] = tile_of(usage_ref, 8, rows_iota((8, LANES)))
    table = tile_of(table_ref, 16, lanes_iota((8, LANES)))
    rows = rows_iota((days, LANES))

    def step(j, _):
        for u in range(STEP // LANES):
            at = lanes_of(j, u)
            gamma = gamma_of(table, index_ref[:, at])
            gamma_ref[:, at] = gamma[:1]
            bound_ref[:, at] = jnp.where(rows < count_ref[:, at], bound_ref[:, at], 0.0)
            w = w_ref[:, at]
            kt_ref[:, at] = w - gamma * jnp.where(rows == days - 1, 0.0, pltpu.roll(w, days - 1, 0))
        return 0

    lax.fori_loop(0, classes // STEP, step, 0)


def first_primal(
    cost_hbm, x_hbm, weights_ref, ends_ref, after_ref, kt_ref, w_ref, inflow_ref, bound_ref, fac_ref, gamma_ref,
    x1_hbm, sum_ref, edge_ref, moved_ref, dual_ref, use_ref, caps_ref, room_ref,
    cost_ref, x_ref, weighted_ref, sems,
):
    days, classes = w_ref.shape
    arrive = block_copies([(cost_hbm, cost_ref), (x_hbm, x_ref)], sems)
    leave = block_copies([(x_ref, x1_hbm)], sems.at[2:])
    start_all(arrive)
    own = caps_ref.shape[1] // ends_ref.shape[0]
    for k in range(ends_ref.shape[0]):
        caps_ref[:, k * own : (k + 1) * own] = ends_ref[k, :, :own]
        room_ref[:, k * own : (k + 1) * own] = ends_ref[k, :, own : 2 * own]
    caps = caps_ref[...]
    weights = weights_ref[...]
    rows = rows_iota((days, LANES))

    def step(j, carry):
        moved, dual = [list(part) for part in carry]
        for u in range(STEP // LANES):
            at = lanes_of(j, u)
            bound = bound_ref[:, at]
            pulled = pulled_of(caps, fac_ref[:, at])
            kt = kt_ref[:, at]
            kt = jnp.where(rows == days - 1, kt - gamma_ref[:, at] * after_ref[:, at], kt)
            sums, weighted = [], []
            for t in range(days):
                old = x_ref[t, :, at]
                grad = cost_ref[t, :, at] - spread(kt, t) - weights * spread(pulled, t)
                new = jnp.minimum(jnp.maximum(old - ETA * grad, 0.0), bound)
                x_ref[t, :, at] = new
                gone = new - old
                moved[u] = moved[u] + gone * gone
                extra = new + gone
                sums.append(extra)
                weighted.append(weights * extra)
            sums = row_sums(sums)
            sum_ref[:, at] = sums
            weighted_ref[:, at] = row_sums(weighted)
            inflow = inflow_ref[:, at]
            edge_ref[:1, at] = sums[days - 1 :]
            edge_ref[1:, at] = w_ref[:1, at] - ETA * (sums[:1] - inflow[:1])
            gap = sums - gamma_ref[:, at] * pltpu.roll(sums, 1, 0) - inflow
            dual[u] = dual[u] + gap * gap
        return tuple(moved), tuple(dual)

    zero = jnp.zeros((8, LANES), F32)
    carry = ((zero,) * (STEP // LANES),) * 2
    each = BLOCK // STEP
    groups = caps_ref.shape[1] // WIDE
    total = jnp.zeros((groups * 3 * days, WIDE), F32)
    for k, block in enumerate(arrive):
        wait_all(block)
        carry = lax.fori_loop(k * each, (k + 1) * each, step, carry)
        start_all(leave[k : k + 1])
        at = pl.ds(k * BLOCK, BLOCK)
        total = total + facility_part(weighted_ref[:, at], fac_ref[:, at], groups)
    moved, dual = [sum(part[1:], part[0]) for part in carry]
    moved_ref[...] = moved
    dual_ref[...] = jnp.where(rows > 0, (ETA * ETA) * dual, 0.0)
    for g, part in enumerate(facility_groups(total, days)):
        use_ref[:, g * WIDE : (g + 1) * WIDE] = part
    for block in leave:
        wait_all(block)


def second_core():
    return lax.rem(lax.axis_index("day"), 2) == 1


def first_send(
    use_ref, moved_ref, dual_ref, chip_ref, far_ref, sum_ref, inflow_ref, gamma_ref, out_ref, prior_ref
):
    days, classes = sum_ref.shape
    second = second_core()
    total = jnp.zeros((1, PART), F32)
    for k in range(classes // PART):
        at = pl.ds(k * PART, PART)
        prior = jnp.where(second, chip_ref[:1, at], far_ref[:1, at])
        prior_ref[:, at] = prior
        gap = sum_ref[:1, at] - gamma_ref[:, at] * prior - inflow_ref[:1, at]
        total = total + gap * gap
    edge = (ETA * ETA) * folded(total)
    dual = dual_ref[...] + jnp.where(rows_iota((days, LANES)) == 0, edge, 0.0)
    use = use_ref[...]
    moved = moved_ref[...]
    for k in range(out_ref.shape[0]):
        out_ref[k, :days, :] = use
        out_ref[k, days:, :LANES] = moved
        out_ref[k, days:, LANES:] = dual


def caps_step(in_ref, caps_ref, room_ref, caps1_ref, out_ref):
    days = caps_ref.shape[0]
    total = in_ref[0]
    for k in range(1, in_ref.shape[0]):
        total = total + in_ref[k]
    caps = caps_ref[...]
    new = jnp.minimum(caps - ETA * (total[:days] - room_ref[...]), 0.0)
    caps1_ref[...] = new
    gone = new - caps
    primal = jnp.sum(total[days:, :LANES], axis=0, keepdims=True)
    dual = jnp.sum(total[days:, LANES:] + folded(gone * gone), axis=0, keepdims=True)
    for k in range(out_ref.shape[0]):
        out_ref[k, :, :LANES] = primal
        out_ref[k, :, LANES:] = dual


def next_duals(w_ref, sum_ref, inflow_ref, gamma_ref, prior_ref, chip_ref, far_ref, w1_ref, kt_ref):
    days, classes = w_ref.shape
    rows = rows_iota((days, LANES))
    second = second_core()
    more = jnp.where(lax.axis_index("day") == lax.axis_size("day") - 1, F32(0.0), F32(ETA))
    for k in range(classes // LANES):
        at = pl.ds(k * LANES, LANES)
        gamma = gamma_ref[:, at]
        sums = sum_ref[:, at]
        prior = jnp.where(rows == 0, prior_ref[:, at], pltpu.roll(sums, 1, 0))
        w = w_ref[:, at] - ETA * (sums - gamma * prior - inflow_ref[:, at])
        w1_ref[:, at] = w
        lead = jnp.where(second, far_ref[1:, at], chip_ref[1:, at])
        edge = lead + more * (gamma * sums[days - 1 :])
        kt_ref[:, at] = w - gamma * jnp.where(rows == days - 1, edge, pltpu.roll(w, days - 1, 0))


def next_grad(cost_hbm, weights_ref, caps_ref, kt_ref, fac_ref, grad_ref, sems):
    days, classes = kt_ref.shape
    arrive = block_copies([(cost_hbm, grad_ref)], sems)
    start_all(arrive)
    caps = caps_ref[...]
    weights = weights_ref[...]

    def step(j, _):
        for u in range(STEP // LANES):
            at = lanes_of(j, u)
            pulled = pulled_of(caps, fac_ref[:, at])
            kt = kt_ref[:, at]
            for t in range(days):
                grad_ref[t, :, at] = grad_ref[t, :, at] - spread(kt, t) - weights * spread(pulled, t)
        return 0

    each = BLOCK // STEP
    for k, block in enumerate(arrive):
        wait_all(block)
        lax.fori_loop(k * each, (k + 1) * each, step, 0)


def second_primal(
    x_hbm, moved_ref, weights_ref, grad_ref, bound_ref, fac_ref, caps_ref,
    x2_hbm, sum_ref, last_ref, omega_ref, out_ref,
    x_ref, weighted_ref, sems,
):
    days, classes = sum_ref.shape
    arrive = block_copies([(x_hbm, x_ref)], sems)
    leave = block_copies([(x_ref, x2_hbm)], sems.at[1:])
    start_all(arrive)
    total = moved_ref[0]
    for k in range(1, moved_ref.shape[0]):
        total = total + moved_ref[k]
    primal = jnp.sum(total[:, :LANES], axis=1, keepdims=True)
    dual = jnp.sum(total[:, LANES:], axis=1, keepdims=True)
    omega = jnp.sqrt(jnp.sqrt((dual + EPS) / (primal + EPS)))
    omega_ref[...] = jnp.broadcast_to(omega, omega_ref.shape)
    tau = jnp.broadcast_to(ETA / omega, (8, LANES))
    weights = weights_ref[...]

    def step(j, _):
        for u in range(STEP // LANES):
            at = lanes_of(j, u)
            bound = bound_ref[:, at]
            sums, weighted = [], []
            for t in range(days):
                old = x_ref[t, :, at]
                new = jnp.minimum(jnp.maximum(old - tau * grad_ref[t, :, at], 0.0), bound)
                x_ref[t, :, at] = new
                extra = new + (new - old)
                sums.append(extra)
                weighted.append(weights * extra)
            sums = row_sums(sums)
            sum_ref[:, at] = sums
            weighted_ref[:, at] = row_sums(weighted)
            last_ref[:, at] = sums[days - 1 :]
        return 0

    each = BLOCK // STEP
    groups = caps_ref.shape[1] // WIDE
    total = jnp.zeros((groups * 3 * days, WIDE), F32)
    for k, block in enumerate(arrive):
        wait_all(block)
        lax.fori_loop(k * each, (k + 1) * each, step, 0)
        start_all(leave[k : k + 1])
        at = pl.ds(k * BLOCK, BLOCK)
        total = total + facility_part(weighted_ref[:, at], fac_ref[:, at], groups)
    parts = facility_groups(total, days)
    own = caps_ref.shape[1] // out_ref.shape[0]
    out_ref[...] = jnp.zeros(out_ref.shape, F32)
    for k in range(out_ref.shape[0]):
        g, place = divmod(k * own, WIDE)
        out_ref[k, :, :own] = parts[g][:, place : place + own]
        out_ref[k, :, own : 2 * own] = caps_ref[:, k * own : (k + 1) * own]
    for block in leave:
        wait_all(block)


def last_duals(in_ref, room_ref, omega_ref, w_ref, sum_ref, prior_ref, inflow_ref, gamma_ref, w2_ref, caps2_ref):
    days, classes = w_ref.shape
    sigma = ETA * omega_ref[...]
    own = room_ref.shape[1]
    use = in_ref[0, :, :own]
    for k in range(1, in_ref.shape[0]):
        use = use + in_ref[k, :, :own]
    caps2_ref[...] = jnp.minimum(
        in_ref[0, :, own : 2 * own] - sigma[:1, :1] * (use - room_ref[...]), 0.0
    )
    rows = rows_iota((days, LANES))
    for k in range(classes // LANES):
        at = pl.ds(k * LANES, LANES)
        sums = sum_ref[:, at]
        prior = jnp.where(rows == 0, prior_ref[:, at], pltpu.roll(sums, 1, 0))
        w2_ref[:, at] = w_ref[:, at] - sigma * (sums - gamma_ref[:, at] * prior - inflow_ref[:, at])


def to_next(row):
    n = lax.axis_size("day")
    return lax.ppermute(row, "day", [(i, i + 1) for i in range(n - 1)])


def to_previous(row):
    n = lax.axis_size("day")
    return lax.ppermute(row, "day", [(i + 1, i) for i in range(n - 1)])


def swapped(rows, first):
    n = lax.axis_size("day")
    pairs = [(i, i + 1) for i in range(first, n - 1, 2)]
    return lax.ppermute(rows, "day", pairs + [(j, i) for i, j in pairs])


def local(
    cost, x_start, ybal_start, inflow, ycap_start, capacity, upper, facility, option_count,
    decay_index, decay_table, usage,
):
    days, opts, classes = cost.shape
    own = ycap_start.shape[1]
    blocks = lax.axis_size("cls")
    facilities = own * blocks
    fac = facility.reshape(1, classes)
    count = option_count.reshape(1, classes)
    index = decay_index.reshape(1, classes)

    ends, row = call(
        start, "start", [struct(blocks, days, LANES), struct(1, classes)], [ANY] * 3,
        [pltpu.VMEM((days, own), F32), pltpu.VMEM((days, own), F32), pltpu.SemaphoreType.DMA((3,))],
    )(*in_hbm(ycap_start, capacity, ybal_start))
    after = to_previous(row)
    ends = lax.all_to_all(ends, "cls", 0, 0)
    field, rows, row, tile = (
        struct(days, opts, classes), struct(days, classes), struct(1, classes), struct(8, LANES)
    )
    table = struct(days, facilities)
    kt, w, inflow, bound, fac, gamma, weights = call(
        load, "load",
        [rows, rows, rows, struct(opts, classes),
         jax.ShapeDtypeStruct((1, classes), jnp.int32), row, tile],
        [ANY] * 8,
        [pltpu.SMEM((opts,), F32), pltpu.SMEM(decay_table.shape, F32), pltpu.VMEM((1, classes), jnp.int32),
         pltpu.VMEM((1, classes), jnp.int32), pltpu.SemaphoreType.DMA((8,))],
        cost=PASS,
    )(*in_hbm(usage, decay_table, ybal_start, inflow, upper, fac, count, index))
    streams = classes // BLOCK
    x1, sums, edge, moved, dual, use, caps, room = call(
        first_primal, "first_primal",
        [pltpu.HBM(field.shape, F32), rows, struct(2, classes), tile, tile, table, table, table],
        [ANY] * 2 + [VM] * 9,
        [pltpu.VMEM(field.shape, F32), pltpu.VMEM(field.shape, F32), pltpu.VMEM(rows.shape, F32),
         pltpu.SemaphoreType.DMA((3, streams))],
        limit=8, out_specs=[ANY] + [VM] * 7,
    )(*in_hbm(cost, x_start), weights, ends, after, kt, w, inflow, bound, fac, gamma)
    chip = swapped(edge, 0)
    far = swapped(edge, 1)
    sent, prior = call(
        first_send, "first_send", [struct(blocks, 2 * days, facilities), row], [VM] * 8
    )(use, moved, dual, chip, far, sums, inflow, gamma)
    got = lax.all_to_all(sent, "cls", 0, 0)
    caps1, sent = call(
        caps_step, "caps_step", [table, struct(lax.axis_size("day"), 1, 2 * LANES)], [VM] * 3
    )(got, caps, room)
    w1, kt = call(next_duals, "next_duals", [rows, rows], [VM] * 7, cost=PASS)(
        w, sums, inflow, gamma, prior, chip, far
    )
    got = lax.all_to_all(sent, "day", 0, 0)
    (grad,) = call(
        next_grad, "next_grad", [field], [ANY] + [VM] * 4, [pltpu.SemaphoreType.DMA((1, streams))], cost=PASS
    )(*in_hbm(cost), weights, caps1, kt, fac)
    x2, sums2, last2, omega, sent = call(
        second_primal, "second_primal",
        [pltpu.HBM(field.shape, F32), rows, row, tile, struct(blocks, days, LANES)],
        [ANY] + [VM] * 6,
        [pltpu.VMEM(field.shape, F32), pltpu.VMEM(rows.shape, F32), pltpu.SemaphoreType.DMA((2, streams))],
        limit=8, out_specs=[ANY] + [VM] * 4,
    )(*in_hbm(x1), got, weights, grad, bound, fac, caps1)
    prior2 = to_next(last2)
    got = lax.all_to_all(sent, "cls", 0, 0)
    w2, caps2 = call(last_duals, "last_duals", [struct(days, classes), struct(days, own)], [VM] * 8)(
        got, capacity, omega, w1, sums2, prior2, inflow, gamma
    )
    return x2, w2, caps2


def solution(mesh):
    in_specs = (
        P("day", None, "cls"), P("day", None, "cls"), P("day", "cls"), P("day", "cls"),
        P("day", "cls"), P("day", "cls"), P(None, "cls"), P("cls"), P("cls"), P("cls"), P(), P(),
    )
    out_specs = (P("day", None, "cls"), P("day", "cls"), P("day", "cls"))
    return jax.shard_map(local, mesh=mesh, in_specs=in_specs, out_specs=out_specs, check_vma=False)
```

```python
import functools

import jax
import jax.numpy as jnp
from jax import lax
from jax.experimental import pallas as pl
from jax.experimental.pallas import tpu as pltpu
from jax.sharding import PartitionSpec as P

ETA = 0.3
EPS = 1e-6
LANES = 128
STEP = 1024
PART = 1024
BLOCK = 1024
HEAD = 2048
WIDE = 64

VM = pl.BlockSpec(memory_space=pltpu.VMEM)
PASS = pl.CostEstimate(flops=10_000_000, bytes_accessed=8_000_000, transcendentals=0)
ANY = pl.BlockSpec(memory_space=pl.ANY)
F32 = jnp.float32


def struct(*shape):
    return jax.ShapeDtypeStruct(shape, F32)


def call(body, name, outs, ins, scratch=(), cost=None, limit=4, out_specs=None):
    return pl.pallas_call(
        body,
        name=name,
        out_shape=outs,
        in_specs=ins,
        out_specs=out_specs or [VM] * len(outs),
        scratch_shapes=list(scratch),
        compiler_params=pltpu.CompilerParams(vmem_limit_bytes=limit << 20),
        cost_estimate=cost,
    )


def in_hbm(*arrays):
    return [pltpu.with_memory_space_constraint(a, pltpu.HBM) for a in arrays]


def rows_iota(shape):
    return lax.broadcasted_iota(jnp.int32, shape, 0)


def lanes_iota(shape):
    return lax.broadcasted_iota(jnp.int32, shape, 1)


def tile_of(ref, count, index):
    out = jnp.zeros(index.shape, F32)
    for k in range(count):
        out = jnp.where(index == k, ref[k], out)
    return out


def lookup(table, index):
    return jnp.take_along_axis(table, index, axis=1, mode="promise_in_bounds")


def folded(wide):
    out = wide[:, :LANES]
    for k in range(1, wide.shape[1] // LANES):
        out = out + wide[:, k * LANES : (k + 1) * LANES]
    return out


def pulled_of(caps, facility):
    days = caps.shape[0]
    parts = []
    for k in range(facility.shape[1] // LANES):
        own = jnp.broadcast_to(facility[:, k * LANES : (k + 1) * LANES], (days, LANES))
        low = jnp.bitwise_and(own, LANES - 1)
        got = lookup(caps[:, :LANES], low)
        for g in range(1, caps.shape[1] // LANES):
            got = jnp.where(own >= g * LANES, lookup(caps[:, g * LANES : (g + 1) * LANES], low), got)
        parts.append(got)
    return jnp.concatenate(parts, axis=1)


def gamma_of(table, index):
    parts = []
    for k in range(index.shape[1] // LANES):
        own = jnp.broadcast_to(index[:, k * LANES : (k + 1) * LANES], (8, LANES))
        parts.append(lookup(table, own))
    return jnp.concatenate(parts, axis=1)


def facility_part(weighted, facility, groups):
    days, classes = weighted.shape
    top = weighted.astype(jnp.bfloat16).astype(F32)
    rest = weighted - top
    mid = rest.astype(jnp.bfloat16).astype(F32)
    low = rest - mid
    group = jnp.broadcast_to(facility // WIDE, (days, classes))
    rows = []
    for g in range(groups):
        mine = group == g
        rows += [jnp.where(mine, top, 0.0), jnp.where(mine, mid, 0.0), jnp.where(mine, low, 0.0)]
    left = jnp.concatenate(rows, axis=0).astype(jnp.bfloat16)
    within = jnp.broadcast_to(jnp.bitwise_and(facility, WIDE - 1), (WIDE, classes))
    member = jnp.where(within == rows_iota((WIDE, classes)), 1.0, 0.0).astype(jnp.bfloat16)
    return lax.dot_general(left, member, (((1,), (1,)), ((), ())), preferred_element_type=F32)


def facility_groups(total, days):
    parts = [total[k : k + days] for k in range(0, total.shape[0], days)]
    return [parts[k] + parts[k + 1] + parts[k + 2] for k in range(0, len(parts), 3)]


def combined(a, b, mask, distance):
    return jnp.where(mask, a, b) + pltpu.roll(jnp.where(mask, b, a), distance, 0)


def row_sums(tiles):
    rows = rows_iota(tiles[0].shape)
    for distance in (1, 2, 4):
        mask = jnp.bitwise_and(rows, distance) == 0
        tiles = [combined(tiles[k], tiles[k + 1], mask, distance) for k in range(0, len(tiles), 2)]
    return tiles[0]


def start(caps_ref, room_ref, w_ref, out_ref, row_ref, caps, room, sems):
    copies = [
        pltpu.make_async_copy(caps_ref, caps, sems.at[0]),
        pltpu.make_async_copy(room_ref, room, sems.at[1]),
        pltpu.make_async_copy(w_ref.at[pl.ds(0, 1)], row_ref, sems.at[2]),
    ]
    for copy in copies:
        copy.start()
    out_ref[...] = jnp.zeros(out_ref.shape, F32)
    copies[0].wait()
    copies[1].wait()
    own = caps.shape[1]
    for k in range(out_ref.shape[0]):
        out_ref[k, :, :own] = caps[...]
        out_ref[k, :, own : 2 * own] = room[...]
    copies[2].wait()


def lanes_of(j, u):
    return pl.ds(pl.multiple_of(j * STEP, STEP) + u * LANES, LANES)


def block_copies(pairs, sems, first=0):
    classes = pairs[0][0].shape[2]
    return [
        [
            pltpu.make_async_copy(
                a.at[:, :, pl.ds(k * BLOCK, BLOCK)], b.at[:, :, pl.ds(k * BLOCK, BLOCK)], sems.at[n, k]
            )
            for n, (a, b) in enumerate(pairs)
        ]
        for k in range(first, classes // BLOCK)
    ]


def start_all(blocks):
    for block in blocks:
        for copy in block:
            copy.start()


def wait_all(block):
    for copy in block:
        copy.wait()


def load(
    usage_hbm, table_hbm, w_hbm, inflow_hbm, upper_hbm, fac_hbm, count_hbm, index_hbm, cost_hbm, x_hbm,
    cost_ref, x_ref, kt_ref, w_ref, inflow_ref, bound_ref, fac_ref, gamma_ref, weights_ref,
    usage_ref, table_ref, count_ref, index_ref, sems,
):
    days, classes = w_ref.shape
    small = [
        (usage_hbm, usage_ref), (table_hbm, table_ref), (fac_hbm, fac_ref), (count_hbm, count_ref),
        (index_hbm, index_ref), (w_hbm, w_ref), (inflow_hbm, inflow_ref), (upper_hbm, bound_ref),
    ]
    small = [pltpu.make_async_copy(a, b, sems.at[k]) for k, (a, b) in enumerate(small)]
    head = pl.ds(0, HEAD)
    large = [
        pltpu.make_async_copy(a.at[:, :, head], b, sems.at[len(small) + k])
        for k, (a, b) in enumerate(((cost_hbm, cost_ref), (x_hbm, x_ref)))
    ]
    for copy in small + large:
        copy.start()
    for copy in small:
        copy.wait()
    weights_ref[...] = tile_of(usage_ref, 8, rows_iota((8, LANES)))
    table = tile_of(table_ref, 16, lanes_iota((8, LANES)))
    rows = rows_iota((days, LANES))

    def step(j, _):
        for u in range(STEP // LANES):
            at = lanes_of(j, u)
            gamma = gamma_of(table, index_ref[:, at])
            gamma_ref[:, at] = gamma[:1]
            bound_ref[:, at] = jnp.where(rows < count_ref[:, at], bound_ref[:, at], 0.0)
            w = w_ref[:, at]
            kt_ref[:, at] = w - gamma * jnp.where(rows == days - 1, 0.0, pltpu.roll(w, days - 1, 0))
        return 0

    lax.fori_loop(0, classes // STEP, step, 0)
    wait_all(large)


def first_primal(
    cost_hbm, x_hbm, cost_head, x_head, weights_ref, ends_ref, after_ref, kt_ref, w_ref, inflow_ref, bound_ref, fac_ref, gamma_ref,
    x1_hbm, sum_ref, weighted_ref, chip_ref, far_ref, moved_ref, caps_ref, room_ref,
    cost_ref, x_ref, sems,
):
    days, classes = w_ref.shape
    ready = HEAD // BLOCK
    arrive = block_copies([(cost_hbm, cost_ref), (x_hbm, x_ref)], sems, ready)
    leave = block_copies([(x_ref, x1_hbm)], sems.at[2:])
    start_all(arrive)
    own = caps_ref.shape[1] // ends_ref.shape[0]
    for k in range(ends_ref.shape[0]):
        caps_ref[:, k * own : (k + 1) * own] = ends_ref[k, :, :own]
        room_ref[:, k * own : (k + 1) * own] = ends_ref[k, :, own : 2 * own]
    caps = caps_ref[...]
    for k in range(classes // LANES):
        at = pl.ds(k * LANES, LANES)
        sum_ref[:, at] = pulled_of(caps, fac_ref[:, at])
    weights = weights_ref[...]
    second = second_core()

    def step(cost_at, x_at, j, moved):
        moved = list(moved)
        for u in range(STEP // LANES):
            at = lanes_of(j, u)
            bound = bound_ref[:, at]
            late = kt_ref[days - 1 :, at] - gamma_ref[:, at] * after_ref[:, at]
            sums, weighted = [], []
            for t in range(days):
                old = x_at[t, :, at]
                kt = late if t == days - 1 else kt_ref[t : t + 1, at]
                grad = cost_at[t, :, at] - kt - weights * sum_ref[t : t + 1, at]
                new = jnp.minimum(jnp.maximum(old - ETA * grad, 0.0), bound)
                x_ref[t, :, at] = new
                gone = new - old
                moved[u % 2] = moved[u % 2] + gone * gone
                extra = new + gone
                sums.append(extra)
                weighted.append(weights * extra)
            sums = row_sums(sums)
            sum_ref[:, at] = sums
            weighted_ref[:, at] = row_sums(weighted)
            last = sums[days - 1 :]
            lead = w_ref[:1, at] - ETA * (sums[:1] - inflow_ref[:1, at])
            chip_ref[:, at] = jnp.where(second, lead, last)
            far_ref[:, at] = jnp.where(second, last, lead)
        return tuple(moved)

    moved = (jnp.zeros((8, LANES), F32),) * 2
    each = BLOCK // STEP
    for k in range(len(leave)):
        if k >= ready:
            wait_all(arrive[k - ready])
        source = (cost_ref, x_ref) if k >= ready else (cost_head, x_head)
        moved = lax.fori_loop(k * each, (k + 1) * each, functools.partial(step, *source), moved)
        start_all(leave[k : k + 1])
    moved_ref[...] = moved[0] + moved[1]
    for block in leave:
        wait_all(block)


def facility_sums(weighted_ref, fac_ref, facilities):
    days, classes = weighted_ref.shape
    groups = facilities // WIDE
    total = jnp.zeros((groups * 3 * days, WIDE), F32)
    for k in range(classes // PART):
        at = pl.ds(k * PART, PART)
        total = total + facility_part(weighted_ref[:, at], fac_ref[:, at], groups)
    return facility_groups(total, days)


def first_use(weighted_ref, sum_ref, inflow_ref, gamma_ref, fac_ref, use_ref, dual_ref):
    days, classes = sum_ref.shape
    for g, part in enumerate(facility_sums(weighted_ref, fac_ref, use_ref.shape[1])):
        use_ref[:, g * WIDE : (g + 1) * WIDE] = part
    total = jnp.zeros((days, PART), F32)
    for k in range(classes // PART):
        at = pl.ds(k * PART, PART)
        sums = sum_ref[:, at]
        gap = sums - gamma_ref[:, at] * pltpu.roll(sums, 1, 0) - inflow_ref[:, at]
        total = total + gap * gap
    dual_ref[...] = jnp.where(rows_iota((days, LANES)) > 0, (ETA * ETA) * folded(total), 0.0)


def second_core():
    return lax.rem(lax.axis_index("day"), 2) == 1


def first_send(
    use_ref, moved_ref, dual_ref, chip_ref, far_ref, sum_ref, inflow_ref, gamma_ref, out_ref, prior_ref
):
    days, classes = sum_ref.shape
    second = second_core()
    total = jnp.zeros((1, PART), F32)
    for k in range(classes // PART):
        at = pl.ds(k * PART, PART)
        prior = jnp.where(second, chip_ref[:, at], far_ref[:, at])
        prior_ref[:, at] = prior
        gap = sum_ref[:1, at] - gamma_ref[:, at] * prior - inflow_ref[:1, at]
        total = total + gap * gap
    edge = (ETA * ETA) * folded(total)
    dual = dual_ref[...] + jnp.where(rows_iota((days, LANES)) == 0, edge, 0.0)
    use = use_ref[...]
    moved = moved_ref[...]
    for k in range(out_ref.shape[0]):
        out_ref[k, :days, :] = use
        out_ref[k, days:, :LANES] = moved
        out_ref[k, days:, LANES:] = dual


def caps_step(in_ref, caps_ref, room_ref, caps1_ref, out_ref):
    days = caps_ref.shape[0]
    total = in_ref[0]
    for k in range(1, in_ref.shape[0]):
        total = total + in_ref[k]
    caps = caps_ref[...]
    new = jnp.minimum(caps - ETA * (total[:days] - room_ref[...]), 0.0)
    caps1_ref[...] = new
    gone = new - caps
    primal = jnp.sum(total[days:, :LANES], axis=0, keepdims=True)
    dual = jnp.sum(total[days:, LANES:] + folded(gone * gone), axis=0, keepdims=True)
    for k in range(out_ref.shape[0]):
        out_ref[k, :, :LANES] = primal
        out_ref[k, :, LANES:] = dual


def next_duals(w_ref, sum_ref, inflow_ref, gamma_ref, prior_ref, chip_ref, far_ref, w1_ref, kt_ref):
    days, classes = w_ref.shape
    rows = rows_iota((days, LANES))
    second = second_core()
    more = jnp.where(lax.axis_index("day") == lax.axis_size("day") - 1, F32(0.0), F32(ETA))
    for k in range(classes // LANES):
        at = pl.ds(k * LANES, LANES)
        gamma = gamma_ref[:, at]
        sums = sum_ref[:, at]
        prior = jnp.where(rows == 0, prior_ref[:, at], pltpu.roll(sums, 1, 0))
        w = w_ref[:, at] - ETA * (sums - gamma * prior - inflow_ref[:, at])
        w1_ref[:, at] = w
        lead = jnp.where(second, far_ref[:, at], chip_ref[:, at])
        edge = lead + more * (gamma * sums[days - 1 :])
        kt_ref[:, at] = w - gamma * jnp.where(rows == days - 1, edge, pltpu.roll(w, days - 1, 0))


def next_grad(cost_hbm, weights_ref, caps_ref, kt_ref, fac_ref, grad_ref, sems):
    days, classes = kt_ref.shape
    arrive = block_copies([(cost_hbm, grad_ref)], sems)
    start_all(arrive)
    caps = caps_ref[...]
    weights = weights_ref[...]

    def step(j, _):
        for u in range(STEP // LANES):
            at = lanes_of(j, u)
            pulled = pulled_of(caps, fac_ref[:, at])
            for t in range(days):
                grad_ref[t, :, at] = grad_ref[t, :, at] - kt_ref[t : t + 1, at] - weights * pulled[t : t + 1]
        return 0

    each = BLOCK // STEP
    for k, block in enumerate(arrive):
        wait_all(block)
        lax.fori_loop(k * each, (k + 1) * each, step, 0)


def second_primal(
    x_hbm, moved_ref, weights_ref, grad_ref, bound_ref, fac_ref, caps_ref,
    x2_hbm, sum_ref, last_ref, omega_ref, out_ref,
    x_ref, weighted_ref, sems,
):
    days, classes = sum_ref.shape
    arrive = block_copies([(x_hbm, x_ref)], sems)
    leave = block_copies([(x_ref, x2_hbm)], sems.at[1:])
    start_all(arrive)
    total = moved_ref[0]
    for k in range(1, moved_ref.shape[0]):
        total = total + moved_ref[k]
    primal = jnp.sum(total[:, :LANES], axis=1, keepdims=True)
    dual = jnp.sum(total[:, LANES:], axis=1, keepdims=True)
    omega = jnp.sqrt(jnp.sqrt((dual + EPS) / (primal + EPS)))
    omega_ref[...] = jnp.broadcast_to(omega, omega_ref.shape)
    tau = jnp.broadcast_to(ETA / omega, (8, LANES))
    weights = weights_ref[...]

    def step(j, _):
        for u in range(STEP // LANES):
            at = lanes_of(j, u)
            bound = bound_ref[:, at]
            sums, weighted = [], []
            for t in range(days):
                old = x_ref[t, :, at]
                new = jnp.minimum(jnp.maximum(old - tau * grad_ref[t, :, at], 0.0), bound)
                x_ref[t, :, at] = new
                extra = new + (new - old)
                sums.append(extra)
                weighted.append(weights * extra)
            sums = row_sums(sums)
            sum_ref[:, at] = sums
            weighted_ref[:, at] = row_sums(weighted)
            last_ref[:, at] = sums[days - 1 :]
        return 0

    each = BLOCK // STEP
    for k, block in enumerate(arrive):
        wait_all(block)
        lax.fori_loop(k * each, (k + 1) * each, step, 0)
        start_all(leave[k : k + 1])
    parts = facility_sums(weighted_ref, fac_ref, caps_ref.shape[1])
    own = caps_ref.shape[1] // out_ref.shape[0]
    out_ref[...] = jnp.zeros(out_ref.shape, F32)
    for k in range(out_ref.shape[0]):
        g, place = divmod(k * own, WIDE)
        out_ref[k, :, :own] = parts[g][:, place : place + own]
        out_ref[k, :, own : 2 * own] = caps_ref[:, k * own : (k + 1) * own]
    for block in leave:
        wait_all(block)


def last_duals(in_ref, room_ref, omega_ref, w_ref, sum_ref, prior_ref, inflow_ref, gamma_ref, w2_ref, caps2_ref):
    days, classes = w_ref.shape
    sigma = ETA * omega_ref[...]
    own = room_ref.shape[1]
    use = in_ref[0, :, :own]
    for k in range(1, in_ref.shape[0]):
        use = use + in_ref[k, :, :own]
    caps2_ref[...] = jnp.minimum(
        in_ref[0, :, own : 2 * own] - sigma[:1, :1] * (use - room_ref[...]), 0.0
    )
    rows = rows_iota((days, LANES))
    for k in range(classes // LANES):
        at = pl.ds(k * LANES, LANES)
        sums = sum_ref[:, at]
        prior = jnp.where(rows == 0, prior_ref[:, at], pltpu.roll(sums, 1, 0))
        w2_ref[:, at] = w_ref[:, at] - sigma * (sums - gamma_ref[:, at] * prior - inflow_ref[:, at])


def to_next(row):
    n = lax.axis_size("day")
    return lax.ppermute(row, "day", [(i, i + 1) for i in range(n - 1)])


def to_previous(row):
    n = lax.axis_size("day")
    return lax.ppermute(row, "day", [(i + 1, i) for i in range(n - 1)])


def swapped(rows, first):
    n = lax.axis_size("day")
    pairs = [(i, i + 1) for i in range(first, n - 1, 2)]
    return lax.ppermute(rows, "day", pairs + [(j, i) for i, j in pairs])


def local(
    cost, x_start, ybal_start, inflow, ycap_start, capacity, upper, facility, option_count,
    decay_index, decay_table, usage,
):
    days, opts, classes = cost.shape
    own = ycap_start.shape[1]
    blocks = lax.axis_size("cls")
    facilities = own * blocks
    fac = facility.reshape(1, classes)
    count = option_count.reshape(1, classes)
    index = decay_index.reshape(1, classes)

    ends, row = call(
        start, "start", [struct(blocks, days, LANES), struct(1, classes)], [ANY] * 3,
        [pltpu.VMEM((days, own), F32), pltpu.VMEM((days, own), F32), pltpu.SemaphoreType.DMA((3,))],
    )(*in_hbm(ycap_start, capacity, ybal_start))
    after = to_previous(row)
    ends = lax.all_to_all(ends, "cls", 0, 0)
    field, rows, row, tile = (
        struct(days, opts, classes), struct(days, classes), struct(1, classes), struct(8, LANES)
    )
    table = struct(days, facilities)
    head = struct(days, opts, HEAD)
    cost_head, x_head, kt, w, inflow, bound, fac, gamma, weights = call(
        load, "load",
        [head, head, rows, rows, rows, struct(opts, classes),
         jax.ShapeDtypeStruct((1, classes), jnp.int32), row, tile],
        [ANY] * 10,
        [pltpu.SMEM((opts,), F32), pltpu.SMEM(decay_table.shape, F32), pltpu.VMEM((1, classes), jnp.int32),
         pltpu.VMEM((1, classes), jnp.int32), pltpu.SemaphoreType.DMA((10,))],
        cost=PASS,
    )(*in_hbm(usage, decay_table, ybal_start, inflow, upper, fac, count, index, cost, x_start))
    streams = classes // BLOCK
    x1, sums, weighted, chip, far, moved, caps, room = call(
        first_primal, "first_primal",
        [pltpu.HBM(field.shape, F32), rows, rows, row, row, tile, table, table],
        [ANY] * 2 + [VM] * 11,
        [pltpu.VMEM(field.shape, F32), pltpu.VMEM(field.shape, F32), pltpu.SemaphoreType.DMA((3, streams))],
        limit=8, out_specs=[ANY] + [VM] * 7,
    )(*in_hbm(cost, x_start), cost_head, x_head, weights, ends, after, kt, w, inflow, bound, fac, gamma)
    chip = swapped(chip, 0)
    far = swapped(far, 1)
    use, dual = call(first_use, "first_use", [table, tile], [VM] * 5, cost=PASS)(
        weighted, sums, inflow, gamma, fac
    )
    sent, prior = call(
        first_send, "first_send", [struct(blocks, 2 * days, facilities), row], [VM] * 8
    )(use, moved, dual, chip, far, sums, inflow, gamma)
    got = lax.all_to_all(sent, "cls", 0, 0)
    caps1, sent = call(
        caps_step, "caps_step", [table, struct(lax.axis_size("day"), 1, 2 * LANES)], [VM] * 3
    )(got, caps, room)
    w1, kt = call(next_duals, "next_duals", [rows, rows], [VM] * 7, cost=PASS)(
        w, sums, inflow, gamma, prior, chip, far
    )
    got = lax.all_to_all(sent, "day", 0, 0)
    (grad,) = call(
        next_grad, "next_grad", [field], [ANY] + [VM] * 4, [pltpu.SemaphoreType.DMA((1, streams))], cost=PASS
    )(*in_hbm(cost), weights, caps1, kt, fac)
    x2, sums2, last2, omega, sent = call(
        second_primal, "second_primal",
        [pltpu.HBM(field.shape, F32), rows, row, tile, struct(blocks, days, LANES)],
        [ANY] + [VM] * 6,
        [pltpu.VMEM(field.shape, F32), pltpu.VMEM(rows.shape, F32), pltpu.SemaphoreType.DMA((2, streams))],
        limit=8, out_specs=[ANY] + [VM] * 4,
    )(*in_hbm(x1), got, weights, grad, bound, fac, caps1)
    prior2 = to_next(last2)
    got = lax.all_to_all(sent, "cls", 0, 0)
    w2, caps2 = call(last_duals, "last_duals", [struct(days, classes), struct(days, own)], [VM] * 8)(
        got, capacity, omega, w1, sums2, prior2, inflow, gamma
    )
    return x2, w2, caps2


def solution(mesh):
    in_specs = (
        P("day", None, "cls"), P("day", None, "cls"), P("day", "cls"), P("day", "cls"),
        P("day", "cls"), P("day", "cls"), P(None, "cls"), P("cls"), P("cls"), P("cls"), P(), P(),
    )
    out_specs = (P("day", None, "cls"), P("day", "cls"), P("day", "cls"))
    return jax.shard_map(local, mesh=mesh, in_specs=in_specs, out_specs=out_specs, check_vma=False)
```

```python
import functools

import jax
import jax.numpy as jnp
from jax import lax
from jax.experimental import pallas as pl
from jax.experimental.pallas import tpu as pltpu
from jax.sharding import PartitionSpec as P

ETA = 0.3
EPS = 1e-6
LANES = 128
STEP = 1024
PART = 1024
BLOCK = 1024
HEAD = 2048
WIDE = 64

VM = pl.BlockSpec(memory_space=pltpu.VMEM)
PASS = pl.CostEstimate(flops=10_000_000, bytes_accessed=8_000_000, transcendentals=0)
ANY = pl.BlockSpec(memory_space=pl.ANY)
F32 = jnp.float32


def struct(*shape):
    return jax.ShapeDtypeStruct(shape, F32)


def call(body, name, outs, ins, scratch=(), cost=None, limit=4, out_specs=None):
    return pl.pallas_call(
        body,
        name=name,
        out_shape=outs,
        in_specs=ins,
        out_specs=out_specs or [VM] * len(outs),
        scratch_shapes=list(scratch),
        compiler_params=pltpu.CompilerParams(vmem_limit_bytes=limit << 20),
        cost_estimate=cost,
    )


def in_hbm(*arrays):
    return [pltpu.with_memory_space_constraint(a, pltpu.HBM) for a in arrays]


def rows_iota(shape):
    return lax.broadcasted_iota(jnp.int32, shape, 0)


def lanes_iota(shape):
    return lax.broadcasted_iota(jnp.int32, shape, 1)


def tile_of(ref, count, index):
    out = jnp.zeros(index.shape, F32)
    for k in range(count):
        out = jnp.where(index == k, ref[k], out)
    return out


def lookup(table, index):
    return jnp.take_along_axis(table, index, axis=1, mode="promise_in_bounds")


def folded(wide):
    out = wide[:, :LANES]
    for k in range(1, wide.shape[1] // LANES):
        out = out + wide[:, k * LANES : (k + 1) * LANES]
    return out


def pulled_of(caps, facility):
    days = caps.shape[0]
    parts = []
    for k in range(facility.shape[1] // LANES):
        own = jnp.broadcast_to(facility[:, k * LANES : (k + 1) * LANES], (days, LANES))
        low = jnp.bitwise_and(own, LANES - 1)
        got = lookup(caps[:, :LANES], low)
        for g in range(1, caps.shape[1] // LANES):
            got = jnp.where(own >= g * LANES, lookup(caps[:, g * LANES : (g + 1) * LANES], low), got)
        parts.append(got)
    return jnp.concatenate(parts, axis=1)


def gamma_of(table, index):
    parts = []
    for k in range(index.shape[1] // LANES):
        own = jnp.broadcast_to(index[:, k * LANES : (k + 1) * LANES], (8, LANES))
        parts.append(lookup(table, own))
    return jnp.concatenate(parts, axis=1)


def facility_part(weighted, facility, groups):
    days, classes = weighted.shape
    top = weighted.astype(jnp.bfloat16).astype(F32)
    rest = weighted - top
    mid = rest.astype(jnp.bfloat16).astype(F32)
    low = rest - mid
    group = jnp.broadcast_to(facility // WIDE, (days, classes))
    rows = []
    for g in range(groups):
        mine = group == g
        rows += [jnp.where(mine, top, 0.0), jnp.where(mine, mid, 0.0), jnp.where(mine, low, 0.0)]
    left = jnp.concatenate(rows, axis=0).astype(jnp.bfloat16)
    within = jnp.broadcast_to(jnp.bitwise_and(facility, WIDE - 1), (WIDE, classes))
    member = jnp.where(within == rows_iota((WIDE, classes)), 1.0, 0.0).astype(jnp.bfloat16)
    return lax.dot_general(left, member, (((1,), (1,)), ((), ())), preferred_element_type=F32)


def facility_groups(total, days):
    parts = [total[k : k + days] for k in range(0, total.shape[0], days)]
    return [parts[k] + parts[k + 1] + parts[k + 2] for k in range(0, len(parts), 3)]


def combined(a, b, mask, distance):
    return jnp.where(mask, a, b) + pltpu.roll(jnp.where(mask, b, a), distance, 0)


def row_sums(tiles):
    rows = rows_iota(tiles[0].shape)
    for distance in (1, 2, 4):
        mask = jnp.bitwise_and(rows, distance) == 0
        tiles = [combined(tiles[k], tiles[k + 1], mask, distance) for k in range(0, len(tiles), 2)]
    return tiles[0]


def flat(tile):
    return jnp.concatenate([tile[t : t + 1] for t in range(tile.shape[0])], axis=1)


def unflat(line, rows):
    width = line.shape[1] // rows
    return jnp.concatenate([line[:, t * width : (t + 1) * width] for t in range(rows)], axis=0)


def start(caps_ref, room_ref, w_ref, out_ref, row_ref, caps, room, sems):
    copies = [
        pltpu.make_async_copy(caps_ref, caps, sems.at[0]),
        pltpu.make_async_copy(room_ref, room, sems.at[1]),
        pltpu.make_async_copy(w_ref.at[pl.ds(0, 1)], row_ref, sems.at[2]),
    ]
    for copy in copies:
        copy.start()
    copies[0].wait()
    copies[1].wait()
    line = flat(jnp.concatenate([caps[...], room[...]], axis=1))
    for k in range(out_ref.shape[0]):
        out_ref[k] = line
    copies[2].wait()


def lanes_of(j, u):
    return pl.ds(pl.multiple_of(j * STEP, STEP) + u * LANES, LANES)


def block_copies(pairs, sems, first=0):
    classes = pairs[0][0].shape[2]
    return [
        [
            pltpu.make_async_copy(
                a.at[:, :, pl.ds(k * BLOCK, BLOCK)], b.at[:, :, pl.ds(k * BLOCK, BLOCK)], sems.at[n, k]
            )
            for n, (a, b) in enumerate(pairs)
        ]
        for k in range(first, classes // BLOCK)
    ]


def start_all(blocks):
    for block in blocks:
        for copy in block:
            copy.start()


def wait_all(block):
    for copy in block:
        copy.wait()


def load(
    usage_hbm, table_hbm, w_hbm, inflow_hbm, upper_hbm, fac_hbm, count_hbm, index_hbm, cost_hbm, x_hbm,
    cost_ref, x_ref, kt_ref, w_ref, inflow_ref, bound_ref, fac_ref, gamma_ref, weights_ref,
    usage_ref, table_ref, count_ref, index_ref, sems,
):
    days, classes = w_ref.shape
    small = [
        (usage_hbm, usage_ref), (table_hbm, table_ref), (fac_hbm, fac_ref), (count_hbm, count_ref),
        (index_hbm, index_ref), (w_hbm, w_ref), (inflow_hbm, inflow_ref), (upper_hbm, bound_ref),
    ]
    small = [pltpu.make_async_copy(a, b, sems.at[k]) for k, (a, b) in enumerate(small)]
    head = pl.ds(0, HEAD)
    large = [
        pltpu.make_async_copy(a.at[:, :, head], b, sems.at[len(small) + k])
        for k, (a, b) in enumerate(((cost_hbm, cost_ref), (x_hbm, x_ref)))
    ]
    for copy in small + large:
        copy.start()
    for copy in small:
        copy.wait()
    weights_ref[...] = tile_of(usage_ref, 8, rows_iota((8, LANES)))
    table = tile_of(table_ref, 16, lanes_iota((8, LANES)))
    rows = rows_iota((days, LANES))

    def step(j, _):
        for u in range(STEP // LANES):
            at = lanes_of(j, u)
            gamma = gamma_of(table, index_ref[:, at])
            gamma_ref[:, at] = gamma[:1]
            bound_ref[:, at] = jnp.where(rows < count_ref[:, at], bound_ref[:, at], 0.0)
            w = w_ref[:, at]
            kt_ref[:, at] = w - gamma * jnp.where(rows == days - 1, 0.0, pltpu.roll(w, days - 1, 0))
        return 0

    lax.fori_loop(0, classes // STEP, step, 0)
    wait_all(large)


def first_primal(
    cost_hbm, x_hbm, cost_head, x_head, weights_ref, ends_ref, after_ref, kt_ref, w_ref, inflow_ref, bound_ref, fac_ref, gamma_ref,
    x1_hbm, sum_ref, weighted_ref, chip_ref, far_ref, moved_ref, caps_ref, room_ref,
    cost_ref, x_ref, sems,
):
    days, classes = w_ref.shape
    ready = HEAD // BLOCK
    arrive = block_copies([(cost_hbm, cost_ref), (x_hbm, x_ref)], sems, ready)
    leave = block_copies([(x_ref, x1_hbm)], sems.at[2:])
    start_all(arrive)
    own = caps_ref.shape[1] // ends_ref.shape[0]
    for k in range(ends_ref.shape[0]):
        ends = unflat(ends_ref[k], days)
        caps_ref[:, k * own : (k + 1) * own] = ends[:, :own]
        room_ref[:, k * own : (k + 1) * own] = ends[:, own:]
    caps = caps_ref[...]
    for k in range(classes // LANES):
        at = pl.ds(k * LANES, LANES)
        sum_ref[:, at] = pulled_of(caps, fac_ref[:, at])
    weights = weights_ref[...]
    second = second_core()

    def step(cost_at, x_at, j, moved):
        moved = list(moved)
        for u in range(STEP // LANES):
            at = lanes_of(j, u)
            bound = bound_ref[:, at]
            late = kt_ref[days - 1 :, at] - gamma_ref[:, at] * after_ref[:, at]
            sums, weighted = [], []
            for t in range(days):
                old = x_at[t, :, at]
                kt = late if t == days - 1 else kt_ref[t : t + 1, at]
                grad = cost_at[t, :, at] - kt - weights * sum_ref[t : t + 1, at]
                new = jnp.minimum(jnp.maximum(old - ETA * grad, 0.0), bound)
                x_ref[t, :, at] = new
                gone = new - old
                moved[u % 2] = moved[u % 2] + gone * gone
                extra = new + gone
                sums.append(extra)
                weighted.append(weights * extra)
            sums = row_sums(sums)
            sum_ref[:, at] = sums
            weighted_ref[:, at] = row_sums(weighted)
            last = sums[days - 1 :]
            lead = w_ref[:1, at] - ETA * (sums[:1] - inflow_ref[:1, at])
            chip_ref[:, at] = jnp.where(second, lead, last)
            far_ref[:, at] = jnp.where(second, last, lead)
        return tuple(moved)

    moved = (jnp.zeros((8, LANES), F32),) * 2
    each = BLOCK // STEP
    for k in range(len(leave)):
        if k >= ready:
            wait_all(arrive[k - ready])
        source = (cost_ref, x_ref) if k >= ready else (cost_head, x_head)
        moved = lax.fori_loop(k * each, (k + 1) * each, functools.partial(step, *source), moved)
        start_all(leave[k : k + 1])
    moved_ref[...] = moved[0] + moved[1]
    for block in leave:
        wait_all(block)


def facility_sums(weighted_ref, fac_ref, facilities):
    days, classes = weighted_ref.shape
    groups = facilities // WIDE
    total = jnp.zeros((groups * 3 * days, WIDE), F32)
    for k in range(classes // PART):
        at = pl.ds(k * PART, PART)
        total = total + facility_part(weighted_ref[:, at], fac_ref[:, at], groups)
    return facility_groups(total, days)


def first_use(weighted_ref, sum_ref, inflow_ref, gamma_ref, fac_ref, use_ref, dual_ref):
    days, classes = sum_ref.shape
    for g, part in enumerate(facility_sums(weighted_ref, fac_ref, use_ref.shape[1])):
        use_ref[:, g * WIDE : (g + 1) * WIDE] = part
    total = jnp.zeros((days, PART), F32)
    for k in range(classes // PART):
        at = pl.ds(k * PART, PART)
        sums = sum_ref[:, at]
        gap = sums - gamma_ref[:, at] * pltpu.roll(sums, 1, 0) - inflow_ref[:, at]
        total = total + gap * gap
    dual_ref[...] = jnp.where(rows_iota((days, LANES)) > 0, (ETA * ETA) * folded(total), 0.0)


def second_core():
    return lax.rem(lax.axis_index("day"), 2) == 1


def first_send(
    use_ref, moved_ref, dual_ref, chip_ref, far_ref, sum_ref, inflow_ref, gamma_ref, out_ref, prior_ref
):
    days, classes = sum_ref.shape
    second = second_core()
    total = jnp.zeros((1, PART), F32)
    for k in range(classes // PART):
        at = pl.ds(k * PART, PART)
        prior = jnp.where(second, chip_ref[:, at], far_ref[:, at])
        prior_ref[:, at] = prior
        gap = sum_ref[:1, at] - gamma_ref[:, at] * prior - inflow_ref[:1, at]
        total = total + gap * gap
    edge = (ETA * ETA) * folded(total)
    dual = dual_ref[...] + jnp.where(rows_iota((days, LANES)) == 0, edge, 0.0)
    line = jnp.concatenate(
        [
            flat(use_ref[...]),
            jnp.sum(moved_ref[...], axis=0, keepdims=True),
            jnp.sum(dual, axis=0, keepdims=True),
        ],
        axis=1,
    )
    for k in range(out_ref.shape[0]):
        out_ref[k] = line


def caps_step(in_ref, caps_ref, room_ref, caps1_ref, out_ref):
    days, facilities = caps_ref.shape
    total = in_ref[0]
    for k in range(1, in_ref.shape[0]):
        total = total + in_ref[k]
    uses = days * facilities
    caps = caps_ref[...]
    new = jnp.minimum(caps - ETA * (unflat(total[:, :uses], days) - room_ref[...]), 0.0)
    caps1_ref[...] = new
    gone = new - caps
    primal = total[:, uses : uses + LANES]
    dual = total[:, uses + LANES :] + jnp.sum(folded(gone * gone), axis=0, keepdims=True)
    for k in range(out_ref.shape[0]):
        out_ref[k, :, :LANES] = primal
        out_ref[k, :, LANES:] = dual


def next_duals(w_ref, sum_ref, inflow_ref, gamma_ref, prior_ref, chip_ref, far_ref, w1_ref, kt_ref):
    days, classes = w_ref.shape
    rows = rows_iota((days, LANES))
    second = second_core()
    more = jnp.where(lax.axis_index("day") == lax.axis_size("day") - 1, F32(0.0), F32(ETA))
    for k in range(classes // LANES):
        at = pl.ds(k * LANES, LANES)
        gamma = gamma_ref[:, at]
        sums = sum_ref[:, at]
        prior = jnp.where(rows == 0, prior_ref[:, at], pltpu.roll(sums, 1, 0))
        w = w_ref[:, at] - ETA * (sums - gamma * prior - inflow_ref[:, at])
        w1_ref[:, at] = w
        lead = jnp.where(second, far_ref[:, at], chip_ref[:, at])
        edge = lead + more * (gamma * sums[days - 1 :])
        kt_ref[:, at] = w - gamma * jnp.where(rows == days - 1, edge, pltpu.roll(w, days - 1, 0))


def next_grad(
    cost_hbm, x_hbm, weights_ref, caps_ref, kt_ref, fac_ref, grad_ref, head_ref, sems, head_sem
):
    days, classes = kt_ref.shape
    arrive = block_copies([(cost_hbm, grad_ref)], sems)
    start_all(arrive)
    head = pltpu.make_async_copy(x_hbm.at[:, :, pl.ds(0, BLOCK)], head_ref, head_sem)
    head.start()
    caps = caps_ref[...]
    weights = weights_ref[...]

    def step(j, _):
        for u in range(STEP // LANES):
            at = lanes_of(j, u)
            pulled = pulled_of(caps, fac_ref[:, at])
            for t in range(days):
                grad_ref[t, :, at] = grad_ref[t, :, at] - kt_ref[t : t + 1, at] - weights * pulled[t : t + 1]
        return 0

    each = BLOCK // STEP
    for k, block in enumerate(arrive):
        wait_all(block)
        lax.fori_loop(k * each, (k + 1) * each, step, 0)
    head.wait()


def second_primal(
    x_hbm, x_head, moved_ref, weights_ref, grad_ref, bound_ref, fac_ref,
    x2_hbm, sum_ref, last_hbm, omega_ref, out_hbm,
    x_ref, weighted_ref, last_ref, out_ref, sems, small_sems,
):
    days, classes = sum_ref.shape
    ready = x_head.shape[2] // BLOCK
    arrive = block_copies([(x_hbm, x_ref)], sems, ready)
    leave = block_copies([(x_ref, x2_hbm)], sems.at[1:])
    start_all(arrive)
    total = moved_ref[0]
    for k in range(1, moved_ref.shape[0]):
        total = total + moved_ref[k]
    primal = jnp.sum(total[:, :LANES], axis=1, keepdims=True)
    dual = jnp.sum(total[:, LANES:], axis=1, keepdims=True)
    omega = jnp.sqrt(jnp.sqrt((dual + EPS) / (primal + EPS)))
    omega_ref[...] = jnp.broadcast_to(omega, omega_ref.shape)
    tau = jnp.broadcast_to(ETA / omega, (8, LANES))
    weights = weights_ref[...]

    def step(x_at, j, _):
        for u in range(STEP // LANES):
            at = lanes_of(j, u)
            bound = bound_ref[:, at]
            sums, weighted = [], []
            for t in range(days):
                old = x_at[t, :, at]
                new = jnp.minimum(jnp.maximum(old - tau * grad_ref[t, :, at], 0.0), bound)
                x_ref[t, :, at] = new
                extra = new + (new - old)
                sums.append(extra)
                weighted.append(weights * extra)
            sums = row_sums(sums)
            sum_ref[:, at] = sums
            weighted_ref[:, at] = row_sums(weighted)
            last_ref[:, at] = sums[days - 1 :]
        return 0

    each = BLOCK // STEP
    for k in range(len(leave)):
        if k >= ready:
            wait_all(arrive[k - ready])
        source = x_ref if k >= ready else x_head
        lax.fori_loop(k * each, (k + 1) * each, functools.partial(step, source), 0)
        start_all(leave[k : k + 1])
    row = pltpu.make_async_copy(last_ref, last_hbm, small_sems.at[0])
    row.start()
    blocks = out_ref.shape[0]
    own = out_ref.shape[2] // days
    parts = facility_sums(weighted_ref, fac_ref, own * blocks)
    for k in range(blocks):
        g, place = divmod(k * own, WIDE)
        out_ref[k] = flat(parts[g][:, place : place + own])
    out = pltpu.make_async_copy(out_ref, out_hbm, small_sems.at[1])
    out.start()
    row.wait()
    out.wait()
    for block in leave:
        wait_all(block)


def last_duals(
    in_ref, caps_ref, room_ref, omega_ref, w_ref, sum_ref, prior_ref, inflow_ref, gamma_ref, w2_ref, caps2_ref
):
    days, classes = w_ref.shape
    sigma = ETA * omega_ref[...]
    own = room_ref.shape[1]
    blocks = in_ref.shape[0]
    mine = lax.axis_index("cls")
    use, caps = in_ref[0], caps_ref[:, :own]
    for k in range(1, blocks):
        use = use + in_ref[k]
        caps = jnp.where(mine == k, caps_ref[:, k * own : (k + 1) * own], caps)
    caps2_ref[...] = jnp.minimum(caps - sigma[:1, :1] * (unflat(use, days) - room_ref[...]), 0.0)
    rows = rows_iota((days, LANES))
    for k in range(classes // LANES):
        at = pl.ds(k * LANES, LANES)
        sums = sum_ref[:, at]
        prior = jnp.where(rows == 0, prior_ref[:, at], pltpu.roll(sums, 1, 0))
        w2_ref[:, at] = w_ref[:, at] - sigma * (sums - gamma_ref[:, at] * prior - inflow_ref[:, at])


def to_next(row):
    n = lax.axis_size("day")
    return lax.ppermute(row, "day", [(i, i + 1) for i in range(n - 1)])


def to_previous(row):
    n = lax.axis_size("day")
    return lax.ppermute(row, "day", [(i + 1, i) for i in range(n - 1)])


def swapped(rows, first):
    n = lax.axis_size("day")
    pairs = [(i, i + 1) for i in range(first, n - 1, 2)]
    return lax.ppermute(rows, "day", pairs + [(j, i) for i, j in pairs])


def local(
    cost, x_start, ybal_start, inflow, ycap_start, capacity, upper, facility, option_count,
    decay_index, decay_table, usage,
):
    days, opts, classes = cost.shape
    own = ycap_start.shape[1]
    blocks = lax.axis_size("cls")
    facilities = own * blocks
    fac = facility.reshape(1, classes)
    count = option_count.reshape(1, classes)
    index = decay_index.reshape(1, classes)

    ends, row = call(
        start, "start", [struct(blocks, 1, 2 * days * own), struct(1, classes)], [ANY] * 3,
        [pltpu.VMEM((days, own), F32), pltpu.VMEM((days, own), F32), pltpu.SemaphoreType.DMA((3,))],
    )(*in_hbm(ycap_start, capacity, ybal_start))
    after = to_previous(row)
    ends = lax.all_to_all(ends, "cls", 0, 0)
    field, rows, row, tile = (
        struct(days, opts, classes), struct(days, classes), struct(1, classes), struct(8, LANES)
    )
    table = struct(days, facilities)
    head = struct(days, opts, HEAD)
    cost_head, x_head, kt, w, inflow, bound, fac, gamma, weights = call(
        load, "load",
        [head, head, rows, rows, rows, struct(opts, classes),
         jax.ShapeDtypeStruct((1, classes), jnp.int32), row, tile],
        [ANY] * 10,
        [pltpu.SMEM((opts,), F32), pltpu.SMEM(decay_table.shape, F32), pltpu.VMEM((1, classes), jnp.int32),
         pltpu.VMEM((1, classes), jnp.int32), pltpu.SemaphoreType.DMA((10,))],
        cost=PASS,
    )(*in_hbm(usage, decay_table, ybal_start, inflow, upper, fac, count, index, cost, x_start))
    streams = classes // BLOCK
    x1, sums, weighted, chip, far, moved, caps, room = call(
        first_primal, "first_primal",
        [pltpu.HBM(field.shape, F32), rows, rows, row, row, tile, table, table],
        [ANY] * 2 + [VM] * 11,
        [pltpu.VMEM(field.shape, F32), pltpu.VMEM(field.shape, F32), pltpu.SemaphoreType.DMA((3, streams))],
        limit=8, out_specs=[ANY] + [VM] * 7,
    )(*in_hbm(cost, x_start), cost_head, x_head, weights, ends, after, kt, w, inflow, bound, fac, gamma)
    chip = swapped(chip, 0)
    far = swapped(far, 1)
    use, dual = call(first_use, "first_use", [table, tile], [VM] * 5, cost=PASS)(
        weighted, sums, inflow, gamma, fac
    )
    sent, prior = call(
        first_send, "first_send", [struct(blocks, 1, days * facilities + 2 * LANES), row], [VM] * 8
    )(use, moved, dual, chip, far, sums, inflow, gamma)
    got = lax.all_to_all(sent, "cls", 0, 0)
    caps1, sent = call(
        caps_step, "caps_step", [table, struct(lax.axis_size("day"), 1, 2 * LANES)], [VM] * 3
    )(got, caps, room)
    w1, kt = call(next_duals, "next_duals", [rows, rows], [VM] * 7, cost=PASS)(
        w, sums, inflow, gamma, prior, chip, far
    )
    got = lax.all_to_all(sent, "day", 0, 0)
    grad, x1_head = call(
        next_grad, "next_grad", [field, struct(days, opts, BLOCK)], [ANY] * 2 + [VM] * 4,
        [pltpu.SemaphoreType.DMA((1, streams)), pltpu.SemaphoreType.DMA], cost=PASS,
    )(*in_hbm(cost, x1), weights, caps1, kt, fac)
    x2, sums2, last2, omega, sent = call(
        second_primal, "second_primal",
        [pltpu.HBM(field.shape, F32), rows, pltpu.HBM(row.shape, F32), tile,
         pltpu.HBM((blocks, 1, days * own), F32)],
        [ANY] + [VM] * 6,
        [pltpu.VMEM(field.shape, F32), pltpu.VMEM(rows.shape, F32), pltpu.VMEM(row.shape, F32),
         pltpu.VMEM((blocks, 1, days * own), F32), pltpu.SemaphoreType.DMA((2, streams)),
         pltpu.SemaphoreType.DMA((2,))],
        limit=8, out_specs=[ANY, VM, ANY, VM, ANY],
    )(*in_hbm(x1), x1_head, got, weights, grad, bound, fac)
    prior2 = to_next(last2)
    got = lax.all_to_all(sent, "cls", 0, 0)
    w2, caps2 = call(last_duals, "last_duals", [struct(days, classes), struct(days, own)], [VM] * 9)(
        got, caps1, capacity, omega, w1, sums2, prior2, inflow, gamma
    )
    return x2, w2, caps2


def solution(mesh):
    in_specs = (
        P("day", None, "cls"), P("day", None, "cls"), P("day", "cls"), P("day", "cls"),
        P("day", "cls"), P("day", "cls"), P(None, "cls"), P("cls"), P("cls"), P("cls"), P(), P(),
    )
    out_specs = (P("day", None, "cls"), P("day", "cls"), P("day", "cls"))
    return jax.shard_map(local, mesh=mesh, in_specs=in_specs, out_specs=out_specs, check_vma=False)
```

```python
import functools

import jax
import jax.numpy as jnp
from jax import lax
from jax.experimental import pallas as pl
from jax.experimental.pallas import tpu as pltpu
from jax.sharding import PartitionSpec as P

ETA = 0.3
EPS = 1e-6
LANES = 128
STEP = 1024
PART = 1024
BLOCK = 1024
HEAD = 2048
WIDE = 64

VM = pl.BlockSpec(memory_space=pltpu.VMEM)
PASS = pl.CostEstimate(flops=10_000_000, bytes_accessed=8_000_000, transcendentals=0)
LONG = pl.CostEstimate(flops=10_000_000, bytes_accessed=100_000_000, transcendentals=0)
ANY = pl.BlockSpec(memory_space=pl.ANY)
F32 = jnp.float32


def struct(*shape):
    return jax.ShapeDtypeStruct(shape, F32)


def call(body, name, outs, ins, scratch=(), cost=None, limit=4, out_specs=None):
    return pl.pallas_call(
        body,
        name=name,
        out_shape=outs,
        in_specs=ins,
        out_specs=out_specs or [VM] * len(outs),
        scratch_shapes=list(scratch),
        compiler_params=pltpu.CompilerParams(vmem_limit_bytes=limit << 20),
        cost_estimate=cost,
    )


def in_hbm(*arrays):
    return [pltpu.with_memory_space_constraint(a, pltpu.HBM) for a in arrays]


def rows_iota(shape):
    return lax.broadcasted_iota(jnp.int32, shape, 0)


def lanes_iota(shape):
    return lax.broadcasted_iota(jnp.int32, shape, 1)


def tile_of(ref, count, index):
    out = jnp.zeros(index.shape, F32)
    for k in range(count):
        out = jnp.where(index == k, ref[k], out)
    return out


def lookup(table, index):
    return jnp.take_along_axis(table, index, axis=1, mode="promise_in_bounds")


def folded(wide):
    out = wide[:, :LANES]
    for k in range(1, wide.shape[1] // LANES):
        out = out + wide[:, k * LANES : (k + 1) * LANES]
    return out


def pulled_of(caps, facility):
    days = caps.shape[0]
    parts = []
    for k in range(facility.shape[1] // LANES):
        own = jnp.broadcast_to(facility[:, k * LANES : (k + 1) * LANES], (days, LANES))
        low = jnp.bitwise_and(own, LANES - 1)
        got = lookup(caps[:, :LANES], low)
        for g in range(1, caps.shape[1] // LANES):
            got = jnp.where(own >= g * LANES, lookup(caps[:, g * LANES : (g + 1) * LANES], low), got)
        parts.append(got)
    return jnp.concatenate(parts, axis=1)


def gamma_of(table, index):
    parts = []
    for k in range(index.shape[1] // LANES):
        own = jnp.broadcast_to(index[:, k * LANES : (k + 1) * LANES], (8, LANES))
        parts.append(lookup(table, own))
    return jnp.concatenate(parts, axis=1)


def facility_part(weighted, facility, groups):
    days, classes = weighted.shape
    top = weighted.astype(jnp.bfloat16).astype(F32)
    rest = weighted - top
    mid = rest.astype(jnp.bfloat16).astype(F32)
    low = rest - mid
    group = jnp.broadcast_to(facility // WIDE, (days, classes))
    rows = []
    for g in range(groups):
        mine = group == g
        rows += [jnp.where(mine, top, 0.0), jnp.where(mine, mid, 0.0), jnp.where(mine, low, 0.0)]
    left = jnp.concatenate(rows, axis=0).astype(jnp.bfloat16)
    within = jnp.broadcast_to(jnp.bitwise_and(facility, WIDE - 1), (WIDE, classes))
    member = jnp.where(within == rows_iota((WIDE, classes)), 1.0, 0.0).astype(jnp.bfloat16)
    return lax.dot_general(left, member, (((1,), (1,)), ((), ())), preferred_element_type=F32)


def facility_groups(total, days):
    parts = [total[k : k + days] for k in range(0, total.shape[0], days)]
    return [parts[k] + parts[k + 1] + parts[k + 2] for k in range(0, len(parts), 3)]


def combined(a, b, mask, distance):
    return jnp.where(mask, a, b) + pltpu.roll(jnp.where(mask, b, a), distance, 0)


def row_sums(tiles):
    rows = rows_iota(tiles[0].shape)
    for distance in (1, 2, 4):
        mask = jnp.bitwise_and(rows, distance) == 0
        tiles = [combined(tiles[k], tiles[k + 1], mask, distance) for k in range(0, len(tiles), 2)]
    return tiles[0]


def flat(tile):
    return jnp.concatenate([tile[t : t + 1] for t in range(tile.shape[0])], axis=1)


def unflat(line, rows):
    width = line.shape[1] // rows
    return jnp.concatenate([line[:, t * width : (t + 1) * width] for t in range(rows)], axis=0)


def start(caps_ref, room_ref, w_ref, out_ref, row_ref, caps, room, sems):
    copies = [
        pltpu.make_async_copy(caps_ref, caps, sems.at[0]),
        pltpu.make_async_copy(room_ref, room, sems.at[1]),
        pltpu.make_async_copy(w_ref.at[pl.ds(0, 1)], row_ref, sems.at[2]),
    ]
    for copy in copies:
        copy.start()
    copies[0].wait()
    copies[1].wait()
    own = caps.shape[1]
    out_ref[...] = jnp.zeros(out_ref.shape, F32)
    for k in range(out_ref.shape[0]):
        out_ref[k, :, :own] = caps[...]
        out_ref[k, :, own : 2 * own] = room[...]
    copies[2].wait()


def lanes_of(j, u):
    return pl.ds(pl.multiple_of(j * STEP, STEP) + u * LANES, LANES)


def block_copies(pairs, sems, first=0):
    classes = pairs[0][0].shape[2]
    return [
        [
            pltpu.make_async_copy(
                a.at[:, :, pl.ds(k * BLOCK, BLOCK)], b.at[:, :, pl.ds(k * BLOCK, BLOCK)], sems.at[n, k]
            )
            for n, (a, b) in enumerate(pairs)
        ]
        for k in range(first, classes // BLOCK)
    ]


def start_all(blocks):
    for block in blocks:
        for copy in block:
            copy.start()


def wait_all(block):
    for copy in block:
        copy.wait()


def load(
    usage_hbm, table_hbm, w_hbm, inflow_hbm, upper_hbm, fac_hbm, count_hbm, index_hbm, cost_hbm, x_hbm,
    cost_ref, x_ref, cost_edge, x_edge, kt_ref, w_ref, inflow_ref, bound_ref, fac_ref, gamma_ref, weights_ref,
    usage_ref, table_ref, count_ref, index_ref, sems,
):
    days, classes = w_ref.shape
    small = [
        (usage_hbm, usage_ref), (table_hbm, table_ref), (fac_hbm, fac_ref), (count_hbm, count_ref),
        (index_hbm, index_ref), (w_hbm, w_ref), (inflow_hbm, inflow_ref), (upper_hbm, bound_ref),
    ]
    small = [pltpu.make_async_copy(a, b, sems.at[k]) for k, (a, b) in enumerate(small)]
    head = pl.ds(0, HEAD)
    large = [
        pltpu.make_async_copy(a.at[:, :, head], b, sems.at[len(small) + k])
        for k, (a, b) in enumerate(((cost_hbm, cost_ref), (x_hbm, x_ref)))
    ]
    large += [
        pltpu.make_async_copy(a.at[t], b.at[n], sems.at[len(small) + 2 + 2 * n + k])
        for n, t in enumerate((0, days - 1))
        for k, (a, b) in enumerate(((cost_hbm, cost_edge), (x_hbm, x_edge)))
    ]
    for copy in small + large:
        copy.start()
    for copy in small:
        copy.wait()
    weights_ref[...] = tile_of(usage_ref, 8, rows_iota((8, LANES)))
    table = tile_of(table_ref, 16, lanes_iota((8, LANES)))
    rows = rows_iota((days, LANES))

    def step(j, _):
        for u in range(STEP // LANES):
            at = lanes_of(j, u)
            gamma = gamma_of(table, index_ref[:, at])
            gamma_ref[:, at] = gamma[:1]
            bound_ref[:, at] = jnp.where(rows < count_ref[:, at], bound_ref[:, at], 0.0)
            w = w_ref[:, at]
            kt_ref[:, at] = w - gamma * jnp.where(rows == days - 1, 0.0, pltpu.roll(w, days - 1, 0))
        return 0

    lax.fori_loop(0, classes // STEP, step, 0)
    wait_all(large)


def edge_primal(
    cost_ref, x_ref, weights_ref, ends_ref, after_ref, kt_in_ref, gamma_ref, w_ref, inflow_ref, bound_ref, fac_ref,
    kt_ref, pulled_ref, chip_ref, far_ref, caps_ref, room_ref,
):
    days, classes = w_ref.shape
    own = caps_ref.shape[1] // ends_ref.shape[0]
    for k in range(ends_ref.shape[0]):
        caps_ref[:, k * own : (k + 1) * own] = ends_ref[k, :, :own]
        room_ref[:, k * own : (k + 1) * own] = ends_ref[k, :, own : 2 * own]
    caps = caps_ref[...]
    weights = weights_ref[...]
    second = second_core()
    rows = rows_iota((days, LANES))

    def step(j, _):
        for u in range(STEP // LANES):
            at = lanes_of(j, u)
            pulled = pulled_of(caps, fac_ref[:, at])
            pulled_ref[:, at] = pulled
            kt = kt_in_ref[:, at]
            kt = jnp.where(rows == days - 1, kt - gamma_ref[:, at] * after_ref[:, at], kt)
            kt_ref[:, at] = kt
            sums = []
            for n, t in enumerate((0, days - 1)):
                old = x_ref[n, :, at]
                grad = cost_ref[n, :, at] - kt[t : t + 1] - weights * pulled[t : t + 1]
                new = jnp.minimum(jnp.maximum(old - ETA * grad, 0.0), bound_ref[:, at])
                sums.append(jnp.sum(new + (new - old), axis=0, keepdims=True))
            lead = w_ref[:1, at] - ETA * (sums[0] - inflow_ref[:1, at])
            chip_ref[:, at] = jnp.where(second, lead, sums[1])
            far_ref[:, at] = jnp.where(second, sums[1], lead)
        return 0

    lax.fori_loop(0, classes // STEP, step, 0)


def first_primal(
    cost_hbm, x_hbm, cost_head, x_head, weights_ref, pulled_ref, kt_ref, bound_ref,
    x1_hbm, sum_ref, weighted_ref, moved_ref,
    cost_ref, x_ref, sems,
):
    days, classes = kt_ref.shape
    ready = HEAD // BLOCK
    arrive = block_copies([(cost_hbm, cost_ref), (x_hbm, x_ref)], sems, ready)
    leave = block_copies([(x_ref, x1_hbm)], sems.at[2:])
    start_all(arrive)
    weights = weights_ref[...]

    def step(cost_at, x_at, j, moved):
        moved = list(moved)
        for u in range(STEP // LANES):
            at = lanes_of(j, u)
            bound = bound_ref[:, at]
            sums, weighted = [], []
            for t in range(days):
                old = x_at[t, :, at]
                grad = cost_at[t, :, at] - kt_ref[t : t + 1, at] - weights * pulled_ref[t : t + 1, at]
                new = jnp.minimum(jnp.maximum(old - ETA * grad, 0.0), bound)
                x_ref[t, :, at] = new
                gone = new - old
                moved[u % 2] = moved[u % 2] + gone * gone
                extra = new + gone
                sums.append(extra)
                weighted.append(weights * extra)
            sum_ref[:, at] = row_sums(sums)
            weighted_ref[:, at] = row_sums(weighted)
        return tuple(moved)

    moved = (jnp.zeros((8, LANES), F32),) * 2
    each = BLOCK // STEP
    for k in range(len(leave)):
        if k >= ready:
            wait_all(arrive[k - ready])
        source = (cost_ref, x_ref) if k >= ready else (cost_head, x_head)
        moved = lax.fori_loop(k * each, (k + 1) * each, functools.partial(step, *source), moved)
        start_all(leave[k : k + 1])
    moved_ref[...] = moved[0] + moved[1]
    for block in leave:
        wait_all(block)


def facility_sums(weighted_ref, fac_ref, facilities):
    days, classes = weighted_ref.shape
    groups = facilities // WIDE
    total = jnp.zeros((groups * 3 * days, WIDE), F32)
    for k in range(classes // PART):
        at = pl.ds(k * PART, PART)
        total = total + facility_part(weighted_ref[:, at], fac_ref[:, at], groups)
    return facility_groups(total, days)


def first_use(weighted_ref, sum_ref, inflow_ref, gamma_ref, fac_ref, use_ref, dual_ref):
    days, classes = sum_ref.shape
    for g, part in enumerate(facility_sums(weighted_ref, fac_ref, use_ref.shape[1])):
        use_ref[:, g * WIDE : (g + 1) * WIDE] = part
    total = jnp.zeros((days, PART), F32)
    for k in range(classes // PART):
        at = pl.ds(k * PART, PART)
        sums = sum_ref[:, at]
        gap = sums - gamma_ref[:, at] * pltpu.roll(sums, 1, 0) - inflow_ref[:, at]
        total = total + gap * gap
    dual_ref[...] = jnp.where(rows_iota((days, LANES)) > 0, (ETA * ETA) * folded(total), 0.0)


def second_core():
    return lax.rem(lax.axis_index("day"), 2) == 1


def first_send(
    use_ref, moved_ref, dual_ref, chip_ref, far_ref, sum_ref, inflow_ref, gamma_ref, out_ref, prior_ref
):
    days, classes = sum_ref.shape
    second = second_core()
    total = jnp.zeros((1, PART), F32)
    for k in range(classes // PART):
        at = pl.ds(k * PART, PART)
        prior = jnp.where(second, chip_ref[:, at], far_ref[:, at])
        prior_ref[:, at] = prior
        gap = sum_ref[:1, at] - gamma_ref[:, at] * prior - inflow_ref[:1, at]
        total = total + gap * gap
    edge = (ETA * ETA) * folded(total)
    dual = dual_ref[...] + jnp.where(rows_iota((days, LANES)) == 0, edge, 0.0)
    line = jnp.concatenate(
        [
            flat(use_ref[...]),
            jnp.sum(moved_ref[...], axis=0, keepdims=True),
            jnp.sum(dual, axis=0, keepdims=True),
        ],
        axis=1,
    )
    for k in range(out_ref.shape[0]):
        out_ref[k] = line


def caps_step(in_ref, caps_ref, room_ref, caps1_ref, out_ref):
    days, facilities = caps_ref.shape
    total = in_ref[0]
    for k in range(1, in_ref.shape[0]):
        total = total + in_ref[k]
    uses = days * facilities
    caps = caps_ref[...]
    new = jnp.minimum(caps - ETA * (unflat(total[:, :uses], days) - room_ref[...]), 0.0)
    caps1_ref[...] = new
    gone = new - caps
    primal = total[:, uses : uses + LANES]
    dual = total[:, uses + LANES :] + jnp.sum(folded(gone * gone), axis=0, keepdims=True)
    for k in range(out_ref.shape[0]):
        out_ref[k, :, :LANES] = primal
        out_ref[k, :, LANES:] = dual


def next_duals(w_ref, sum_ref, inflow_ref, gamma_ref, prior_ref, chip_ref, far_ref, w1_ref, kt_ref):
    days, classes = w_ref.shape
    rows = rows_iota((days, LANES))
    second = second_core()
    more = jnp.where(lax.axis_index("day") == lax.axis_size("day") - 1, F32(0.0), F32(ETA))
    for k in range(classes // LANES):
        at = pl.ds(k * LANES, LANES)
        gamma = gamma_ref[:, at]
        sums = sum_ref[:, at]
        prior = jnp.where(rows == 0, prior_ref[:, at], pltpu.roll(sums, 1, 0))
        w = w_ref[:, at] - ETA * (sums - gamma * prior - inflow_ref[:, at])
        w1_ref[:, at] = w
        lead = jnp.where(second, far_ref[:, at], chip_ref[:, at])
        edge = lead + more * (gamma * sums[days - 1 :])
        kt_ref[:, at] = w - gamma * jnp.where(rows == days - 1, edge, pltpu.roll(w, days - 1, 0))


def next_grad(
    cost_hbm, x_hbm, weights_ref, caps_ref, kt_ref, fac_ref, grad_ref, head_ref, sems, head_sem
):
    days, classes = kt_ref.shape
    arrive = block_copies([(cost_hbm, grad_ref)], sems)
    start_all(arrive)
    head = pltpu.make_async_copy(x_hbm.at[:, :, pl.ds(0, BLOCK)], head_ref, head_sem)
    head.start()
    caps = caps_ref[...]
    weights = weights_ref[...]

    def step(j, _):
        for u in range(STEP // LANES):
            at = lanes_of(j, u)
            pulled = pulled_of(caps, fac_ref[:, at])
            for t in range(days):
                grad_ref[t, :, at] = grad_ref[t, :, at] - kt_ref[t : t + 1, at] - weights * pulled[t : t + 1]
        return 0

    each = BLOCK // STEP
    for k, block in enumerate(arrive):
        wait_all(block)
        lax.fori_loop(k * each, (k + 1) * each, step, 0)
    head.wait()


def second_primal(
    x_hbm, x_head, moved_ref, weights_ref, grad_ref, bound_ref, fac_ref, caps_ref,
    x2_hbm, sum_ref, last_hbm, omega_ref, out_hbm,
    x_ref, weighted_ref, last_ref, out_ref, sems, small_sems,
):
    days, classes = sum_ref.shape
    ready = x_head.shape[2] // BLOCK
    arrive = block_copies([(x_hbm, x_ref)], sems, ready)
    leave = block_copies([(x_ref, x2_hbm)], sems.at[1:])
    start_all(arrive)
    total = moved_ref[0]
    for k in range(1, moved_ref.shape[0]):
        total = total + moved_ref[k]
    primal = jnp.sum(total[:, :LANES], axis=1, keepdims=True)
    dual = jnp.sum(total[:, LANES:], axis=1, keepdims=True)
    omega = jnp.sqrt(jnp.sqrt((dual + EPS) / (primal + EPS)))
    omega_ref[...] = jnp.broadcast_to(omega, omega_ref.shape)
    tau = jnp.broadcast_to(ETA / omega, (8, LANES))
    weights = weights_ref[...]

    def step(x_at, j, _):
        for u in range(STEP // LANES):
            at = lanes_of(j, u)
            bound = bound_ref[:, at]
            sums, weighted = [], []
            for t in range(days):
                old = x_at[t, :, at]
                new = jnp.minimum(jnp.maximum(old - tau * grad_ref[t, :, at], 0.0), bound)
                x_ref[t, :, at] = new
                extra = new + (new - old)
                sums.append(extra)
                weighted.append(weights * extra)
            sums = row_sums(sums)
            sum_ref[:, at] = sums
            weighted_ref[:, at] = row_sums(weighted)
            last_ref[:, at] = sums[days - 1 :]
        return 0

    each = BLOCK // STEP
    for k in range(len(leave)):
        if k >= ready:
            wait_all(arrive[k - ready])
        source = x_ref if k >= ready else x_head
        lax.fori_loop(k * each, (k + 1) * each, functools.partial(step, source), 0)
        start_all(leave[k : k + 1])
    row = pltpu.make_async_copy(last_ref, last_hbm, small_sems.at[0])
    row.start()
    blocks = out_ref.shape[0]
    own = caps_ref.shape[1] // blocks
    out_ref[...] = jnp.zeros(out_ref.shape, F32)
    parts = facility_sums(weighted_ref, fac_ref, own * blocks)
    for k in range(blocks):
        g, place = divmod(k * own, WIDE)
        out_ref[k, :, :own] = parts[g][:, place : place + own]
        out_ref[k, :, own : 2 * own] = caps_ref[:, k * own : (k + 1) * own]
    out = pltpu.make_async_copy(out_ref, out_hbm, small_sems.at[1])
    out.start()
    row.wait()
    out.wait()
    for block in leave:
        wait_all(block)


def last_duals(
    in_ref, room_ref, omega_ref, w_ref, sum_ref, prior_ref, inflow_ref, gamma_ref, w2_ref, caps2_ref
):
    days, classes = w_ref.shape
    sigma = ETA * omega_ref[...]
    own = room_ref.shape[1]
    use = in_ref[0, :, :own]
    for k in range(1, in_ref.shape[0]):
        use = use + in_ref[k, :, :own]
    caps2_ref[...] = jnp.minimum(
        in_ref[0, :, own : 2 * own] - sigma[:1, :1] * (use - room_ref[...]), 0.0
    )
    rows = rows_iota((days, LANES))
    for k in range(classes // LANES):
        at = pl.ds(k * LANES, LANES)
        sums = sum_ref[:, at]
        prior = jnp.where(rows == 0, prior_ref[:, at], pltpu.roll(sums, 1, 0))
        w2_ref[:, at] = w_ref[:, at] - sigma * (sums - gamma_ref[:, at] * prior - inflow_ref[:, at])


def to_next(row):
    n = lax.axis_size("day")
    return lax.ppermute(row, "day", [(i, i + 1) for i in range(n - 1)])


def to_previous(row):
    n = lax.axis_size("day")
    return lax.ppermute(row, "day", [(i + 1, i) for i in range(n - 1)])


def swapped(rows, first):
    n = lax.axis_size("day")
    pairs = [(i, i + 1) for i in range(first, n - 1, 2)]
    return lax.ppermute(rows, "day", pairs + [(j, i) for i, j in pairs])


def local(
    cost, x_start, ybal_start, inflow, ycap_start, capacity, upper, facility, option_count,
    decay_index, decay_table, usage,
):
    days, opts, classes = cost.shape
    own = ycap_start.shape[1]
    blocks = lax.axis_size("cls")
    facilities = own * blocks
    fac = facility.reshape(1, classes)
    count = option_count.reshape(1, classes)
    index = decay_index.reshape(1, classes)

    ends, row = call(
        start, "start", [struct(blocks, days, LANES), struct(1, classes)], [ANY] * 3,
        [pltpu.VMEM((days, own), F32), pltpu.VMEM((days, own), F32), pltpu.SemaphoreType.DMA((3,))],
    )(*in_hbm(ycap_start, capacity, ybal_start))
    after = to_previous(row)
    ends = lax.all_to_all(ends, "cls", 0, 0)
    field, rows, row, tile = (
        struct(days, opts, classes), struct(days, classes), struct(1, classes), struct(8, LANES)
    )
    table = struct(days, facilities)
    head = struct(days, opts, HEAD)
    two = struct(2, opts, classes)
    cost_head, x_head, cost_edge, x_edge, kt, w, inflow, bound, fac, gamma, weights = call(
        load, "load",
        [head, head, two, two, rows, rows, rows, struct(opts, classes),
         jax.ShapeDtypeStruct((1, classes), jnp.int32), row, tile],
        [ANY] * 10,
        [pltpu.SMEM((opts,), F32), pltpu.SMEM(decay_table.shape, F32), pltpu.VMEM((1, classes), jnp.int32),
         pltpu.VMEM((1, classes), jnp.int32), pltpu.SemaphoreType.DMA((14,))],
        cost=PASS,
    )(*in_hbm(usage, decay_table, ybal_start, inflow, upper, fac, count, index, cost, x_start))
    streams = classes // BLOCK
    kt, pulled, chip, far, caps, room = call(
        edge_primal, "edge_primal", [rows, rows, row, row, table, table], [VM] * 11
    )(cost_edge, x_edge, weights, ends, after, kt, gamma, w, inflow, bound, fac)
    chip = swapped(chip, 0)
    far = swapped(far, 1)
    x1, sums, weighted, moved = call(
        first_primal, "first_primal", [pltpu.HBM(field.shape, F32), rows, rows, tile], [ANY] * 2 + [VM] * 6,
        [pltpu.VMEM(field.shape, F32), pltpu.VMEM(field.shape, F32), pltpu.SemaphoreType.DMA((3, streams))],
        limit=8, out_specs=[ANY] + [VM] * 3, cost=LONG,
    )(*in_hbm(cost, x_start), cost_head, x_head, weights, pulled, kt, bound)
    use, dual = call(first_use, "first_use", [table, tile], [VM] * 5)(
        weighted, sums, inflow, gamma, fac
    )
    sent, prior = call(
        first_send, "first_send", [struct(blocks, 1, days * facilities + 2 * LANES), row], [VM] * 8
    )(use, moved, dual, chip, far, sums, inflow, gamma)
    got = lax.all_to_all(sent, "cls", 0, 0)
    caps1, sent = call(
        caps_step, "caps_step", [table, struct(lax.axis_size("day"), 1, 2 * LANES)], [VM] * 3
    )(got, caps, room)
    w1, kt = call(next_duals, "next_duals", [rows, rows], [VM] * 7, cost=PASS)(
        w, sums, inflow, gamma, prior, chip, far
    )
    got = lax.all_to_all(sent, "day", 0, 0)
    grad, x1_head = call(
        next_grad, "next_grad", [field, struct(days, opts, BLOCK)], [ANY] * 2 + [VM] * 4,
        [pltpu.SemaphoreType.DMA((1, streams)), pltpu.SemaphoreType.DMA], cost=PASS,
    )(*in_hbm(cost, x1), weights, caps1, kt, fac)
    x2, sums2, last2, omega, sent = call(
        second_primal, "second_primal",
        [pltpu.HBM(field.shape, F32), rows, pltpu.HBM(row.shape, F32), tile,
         pltpu.HBM((blocks, days, LANES), F32)],
        [ANY] + [VM] * 7,
        [pltpu.VMEM(field.shape, F32), pltpu.VMEM(rows.shape, F32), pltpu.VMEM(row.shape, F32),
         pltpu.VMEM((blocks, days, LANES), F32), pltpu.SemaphoreType.DMA((2, streams)),
         pltpu.SemaphoreType.DMA((2,))],
        limit=8, out_specs=[ANY, VM, ANY, VM, ANY],
    )(*in_hbm(x1), x1_head, got, weights, grad, bound, fac, caps1)
    prior2 = to_next(last2)
    got = lax.all_to_all(sent, "cls", 0, 0)
    w2, caps2 = call(last_duals, "last_duals", [struct(days, classes), struct(days, own)], [VM] * 8)(
        got, capacity, omega, w1, sums2, prior2, inflow, gamma
    )
    return x2, w2, caps2


def solution(mesh):
    in_specs = (
        P("day", None, "cls"), P("day", None, "cls"), P("day", "cls"), P("day", "cls"),
        P("day", "cls"), P("day", "cls"), P(None, "cls"), P("cls"), P("cls"), P("cls"), P(), P(),
    )
    out_specs = (P("day", None, "cls"), P("day", "cls"), P("day", "cls"))
    return jax.shard_map(local, mesh=mesh, in_specs=in_specs, out_specs=out_specs, check_vma=False)
```

```python
import functools

import jax
import jax.numpy as jnp
from jax import lax
from jax.experimental import pallas as pl
from jax.experimental.pallas import tpu as pltpu
from jax.sharding import PartitionSpec as P

ETA = 0.3
EPS = 1e-6
LANES = 128
STEP = 1024
PART = 1024
BLOCK = 1024
HEAD = 2048
WIDE = 64

VM = pl.BlockSpec(memory_space=pltpu.VMEM)
PASS = pl.CostEstimate(flops=10_000_000, bytes_accessed=8_000_000, transcendentals=0)
LONG = pl.CostEstimate(flops=10_000_000, bytes_accessed=100_000_000, transcendentals=0)
ANY = pl.BlockSpec(memory_space=pl.ANY)
F32 = jnp.float32


def struct(*shape):
    return jax.ShapeDtypeStruct(shape, F32)


def call(body, name, outs, ins, scratch=(), cost=None, limit=4, out_specs=None):
    return pl.pallas_call(
        body,
        name=name,
        out_shape=outs,
        in_specs=ins,
        out_specs=out_specs or [VM] * len(outs),
        scratch_shapes=list(scratch),
        compiler_params=pltpu.CompilerParams(vmem_limit_bytes=limit << 20),
        cost_estimate=cost,
    )


def in_hbm(*arrays):
    return [pltpu.with_memory_space_constraint(a, pltpu.HBM) for a in arrays]


def rows_iota(shape):
    return lax.broadcasted_iota(jnp.int32, shape, 0)


def lanes_iota(shape):
    return lax.broadcasted_iota(jnp.int32, shape, 1)


def tile_of(ref, count, index):
    out = jnp.zeros(index.shape, F32)
    for k in range(count):
        out = jnp.where(index == k, ref[k], out)
    return out


def lookup(table, index):
    return jnp.take_along_axis(table, index, axis=1, mode="promise_in_bounds")


def folded(wide):
    out = wide[:, :LANES]
    for k in range(1, wide.shape[1] // LANES):
        out = out + wide[:, k * LANES : (k + 1) * LANES]
    return out


def pulled_of(caps, facility):
    days = caps.shape[0]
    parts = []
    for k in range(facility.shape[1] // LANES):
        own = jnp.broadcast_to(facility[:, k * LANES : (k + 1) * LANES], (days, LANES))
        low = jnp.bitwise_and(own, LANES - 1)
        got = lookup(caps[:, :LANES], low)
        for g in range(1, caps.shape[1] // LANES):
            got = jnp.where(own >= g * LANES, lookup(caps[:, g * LANES : (g + 1) * LANES], low), got)
        parts.append(got)
    return jnp.concatenate(parts, axis=1)


def gamma_of(table, index):
    parts = []
    for k in range(index.shape[1] // LANES):
        own = jnp.broadcast_to(index[:, k * LANES : (k + 1) * LANES], (8, LANES))
        parts.append(lookup(table, own))
    return jnp.concatenate(parts, axis=1)


def facility_part(weighted, facility, groups):
    days, classes = weighted.shape
    top = weighted.astype(jnp.bfloat16).astype(F32)
    rest = weighted - top
    mid = rest.astype(jnp.bfloat16).astype(F32)
    low = rest - mid
    group = jnp.broadcast_to(facility // WIDE, (days, classes))
    rows = []
    for g in range(groups):
        mine = group == g
        rows += [jnp.where(mine, top, 0.0), jnp.where(mine, mid, 0.0), jnp.where(mine, low, 0.0)]
    left = jnp.concatenate(rows, axis=0).astype(jnp.bfloat16)
    within = jnp.broadcast_to(jnp.bitwise_and(facility, WIDE - 1), (WIDE, classes))
    member = jnp.where(within == rows_iota((WIDE, classes)), 1.0, 0.0).astype(jnp.bfloat16)
    return lax.dot_general(left, member, (((1,), (1,)), ((), ())), preferred_element_type=F32)


def facility_groups(total, days):
    parts = [total[k : k + days] for k in range(0, total.shape[0], days)]
    return [parts[k] + parts[k + 1] + parts[k + 2] for k in range(0, len(parts), 3)]


def combined(a, b, mask, distance):
    return jnp.where(mask, a, b) + pltpu.roll(jnp.where(mask, b, a), distance, 0)


def row_sums(tiles):
    rows = rows_iota(tiles[0].shape)
    for distance in (1, 2, 4):
        mask = jnp.bitwise_and(rows, distance) == 0
        tiles = [combined(tiles[k], tiles[k + 1], mask, distance) for k in range(0, len(tiles), 2)]
    return tiles[0]


def flat(tile):
    return jnp.concatenate([tile[t : t + 1] for t in range(tile.shape[0])], axis=1)


def unflat(line, rows):
    width = line.shape[1] // rows
    return jnp.concatenate([line[:, t * width : (t + 1) * width] for t in range(rows)], axis=0)


def start(caps_ref, room_ref, w_ref, out_ref, row_ref, caps, room, sems):
    copies = [
        pltpu.make_async_copy(caps_ref, caps, sems.at[0]),
        pltpu.make_async_copy(room_ref, room, sems.at[1]),
        pltpu.make_async_copy(w_ref.at[pl.ds(0, 1)], row_ref, sems.at[2]),
    ]
    for copy in copies:
        copy.start()
    copies[0].wait()
    copies[1].wait()
    own = caps.shape[1]
    out_ref[...] = jnp.zeros(out_ref.shape, F32)
    for k in range(out_ref.shape[0]):
        out_ref[k, :, :own] = caps[...]
        out_ref[k, :, own : 2 * own] = room[...]
    copies[2].wait()


def lanes_of(j, u):
    return pl.ds(pl.multiple_of(j * STEP, STEP) + u * LANES, LANES)


def block_copies(pairs, sems, first=0):
    classes = pairs[0][0].shape[2]
    return [
        [
            pltpu.make_async_copy(
                a.at[:, :, pl.ds(k * BLOCK, BLOCK)], b.at[:, :, pl.ds(k * BLOCK, BLOCK)], sems.at[n, k]
            )
            for n, (a, b) in enumerate(pairs)
        ]
        for k in range(first, classes // BLOCK)
    ]


def start_all(blocks):
    for block in blocks:
        for copy in block:
            copy.start()


def wait_all(block):
    for copy in block:
        copy.wait()


def load(
    usage_hbm, table_hbm, w_hbm, inflow_hbm, upper_hbm, fac_hbm, count_hbm, index_hbm, cost_hbm, x_hbm,
    cost_ref, x_ref, cost_edge, x_edge, kt_ref, w_ref, inflow_ref, bound_ref, fac_ref, gamma_ref, weights_ref,
    usage_ref, table_ref, count_ref, index_ref, sems,
):
    days, classes = w_ref.shape
    small = [
        (usage_hbm, usage_ref), (table_hbm, table_ref), (fac_hbm, fac_ref), (count_hbm, count_ref),
        (index_hbm, index_ref), (w_hbm, w_ref), (inflow_hbm, inflow_ref), (upper_hbm, bound_ref),
    ]
    small = [pltpu.make_async_copy(a, b, sems.at[k]) for k, (a, b) in enumerate(small)]
    head = pl.ds(0, HEAD)
    large = [
        pltpu.make_async_copy(a.at[:, :, head], b, sems.at[len(small) + k])
        for k, (a, b) in enumerate(((cost_hbm, cost_ref), (x_hbm, x_ref)))
    ]
    large += [
        pltpu.make_async_copy(a.at[t], b.at[n], sems.at[len(small) + 2 + 2 * n + k])
        for n, t in enumerate((0, days - 1))
        for k, (a, b) in enumerate(((cost_hbm, cost_edge), (x_hbm, x_edge)))
    ]
    for copy in small + large:
        copy.start()
    for copy in small:
        copy.wait()
    weights_ref[...] = tile_of(usage_ref, 8, rows_iota((8, LANES)))
    table = tile_of(table_ref, 16, lanes_iota((8, LANES)))
    rows = rows_iota((days, LANES))

    def step(j, _):
        for u in range(STEP // LANES):
            at = lanes_of(j, u)
            gamma = gamma_of(table, index_ref[:, at])
            gamma_ref[:, at] = gamma[:1]
            bound_ref[:, at] = jnp.where(rows < count_ref[:, at], bound_ref[:, at], 0.0)
            w = w_ref[:, at]
            kt_ref[:, at] = w - gamma * jnp.where(rows == days - 1, 0.0, pltpu.roll(w, days - 1, 0))
        return 0

    lax.fori_loop(0, classes // STEP, step, 0)
    wait_all(large)


def edge_primal(
    cost_ref, x_ref, weights_ref, ends_ref, after_ref, kt_in_ref, gamma_ref, w_ref, inflow_ref, bound_ref, fac_ref,
    kt_ref, pulled_ref, chip_ref, far_ref, caps_ref, room_ref,
):
    days, classes = w_ref.shape
    own = caps_ref.shape[1] // ends_ref.shape[0]
    for k in range(ends_ref.shape[0]):
        caps_ref[:, k * own : (k + 1) * own] = ends_ref[k, :, :own]
        room_ref[:, k * own : (k + 1) * own] = ends_ref[k, :, own : 2 * own]
    caps = caps_ref[...]
    weights = weights_ref[...]
    second = second_core()
    rows = rows_iota((days, LANES))

    def step(j, _):
        for u in range(STEP // LANES):
            at = lanes_of(j, u)
            pulled = pulled_of(caps, fac_ref[:, at])
            pulled_ref[:, at] = pulled
            kt = kt_in_ref[:, at]
            kt = jnp.where(rows == days - 1, kt - gamma_ref[:, at] * after_ref[:, at], kt)
            kt_ref[:, at] = kt
            sums = []
            for n, t in enumerate((0, days - 1)):
                old = x_ref[n, :, at]
                grad = cost_ref[n, :, at] - kt[t : t + 1] - weights * pulled[t : t + 1]
                new = jnp.minimum(jnp.maximum(old - ETA * grad, 0.0), bound_ref[:, at])
                sums.append(jnp.sum(new + (new - old), axis=0, keepdims=True))
            lead = w_ref[:1, at] - ETA * (sums[0] - inflow_ref[:1, at])
            chip_ref[:, at] = jnp.where(second, lead, sums[1])
            far_ref[:, at] = jnp.where(second, sums[1], lead)
        return 0

    lax.fori_loop(0, classes // STEP, step, 0)


def first_primal(
    cost_hbm, x_hbm, cost_head, x_head, weights_ref, pulled_ref, kt_ref, bound_ref, inflow_ref, gamma_ref, fac_ref,
    x1_hbm, sum_ref, moved_ref, use_ref, dual_ref,
    cost_ref, x_ref, weighted_ref, sems,
):
    days, classes = kt_ref.shape
    ready = HEAD // BLOCK
    arrive = block_copies([(cost_hbm, cost_ref), (x_hbm, x_ref)], sems, ready)
    leave = block_copies([(x_ref, x1_hbm)], sems.at[2:])
    start_all(arrive)
    weights = weights_ref[...]

    def step(cost_at, x_at, j, moved):
        moved = list(moved)
        for u in range(STEP // LANES):
            at = lanes_of(j, u)
            bound = bound_ref[:, at]
            sums, weighted = [], []
            for t in range(days):
                old = x_at[t, :, at]
                grad = cost_at[t, :, at] - kt_ref[t : t + 1, at] - weights * pulled_ref[t : t + 1, at]
                new = jnp.minimum(jnp.maximum(old - ETA * grad, 0.0), bound)
                x_ref[t, :, at] = new
                gone = new - old
                moved[u % 2] = moved[u % 2] + gone * gone
                extra = new + gone
                sums.append(extra)
                weighted.append(weights * extra)
            sum_ref[:, at] = row_sums(sums)
            weighted_ref[:, at] = row_sums(weighted)
        return tuple(moved)

    moved = (jnp.zeros((8, LANES), F32),) * 2
    each = BLOCK // STEP
    for k in range(len(leave)):
        if k >= ready:
            wait_all(arrive[k - ready])
        source = (cost_ref, x_ref) if k >= ready else (cost_head, x_head)
        moved = lax.fori_loop(k * each, (k + 1) * each, functools.partial(step, *source), moved)
        start_all(leave[k : k + 1])
    moved_ref[...] = moved[0] + moved[1]
    interior_use(weighted_ref, sum_ref, inflow_ref, gamma_ref, fac_ref, use_ref, dual_ref)
    for block in leave:
        wait_all(block)


def facility_sums(weighted_ref, fac_ref, facilities):
    days, classes = weighted_ref.shape
    groups = facilities // WIDE
    total = jnp.zeros((groups * 3 * days, WIDE), F32)
    for k in range(classes // PART):
        at = pl.ds(k * PART, PART)
        total = total + facility_part(weighted_ref[:, at], fac_ref[:, at], groups)
    return facility_groups(total, days)


def interior_use(weighted_ref, sum_ref, inflow_ref, gamma_ref, fac_ref, use_ref, dual_ref):
    days, classes = sum_ref.shape
    for g, part in enumerate(facility_sums(weighted_ref, fac_ref, use_ref.shape[1])):
        use_ref[:, g * WIDE : (g + 1) * WIDE] = part
    total = jnp.zeros((days, PART), F32)
    for k in range(classes // PART):
        at = pl.ds(k * PART, PART)
        sums = sum_ref[:, at]
        gap = sums - gamma_ref[:, at] * pltpu.roll(sums, 1, 0) - inflow_ref[:, at]
        total = total + gap * gap
    dual_ref[...] = jnp.where(rows_iota((days, LANES)) > 0, (ETA * ETA) * folded(total), 0.0)


def second_core():
    return lax.rem(lax.axis_index("day"), 2) == 1


def first_send(
    use_ref, moved_ref, dual_ref, chip_ref, far_ref, sum_ref, inflow_ref, gamma_ref, out_ref, prior_ref
):
    days, classes = sum_ref.shape
    second = second_core()
    total = jnp.zeros((1, PART), F32)
    for k in range(classes // PART):
        at = pl.ds(k * PART, PART)
        prior = jnp.where(second, chip_ref[:, at], far_ref[:, at])
        prior_ref[:, at] = prior
        gap = sum_ref[:1, at] - gamma_ref[:, at] * prior - inflow_ref[:1, at]
        total = total + gap * gap
    edge = (ETA * ETA) * folded(total)
    dual = dual_ref[...] + jnp.where(rows_iota((days, LANES)) == 0, edge, 0.0)
    line = jnp.concatenate(
        [
            flat(use_ref[...]),
            jnp.sum(moved_ref[...], axis=0, keepdims=True),
            jnp.sum(dual, axis=0, keepdims=True),
        ],
        axis=1,
    )
    for k in range(out_ref.shape[0]):
        out_ref[k] = line


def caps_step(in_ref, caps_ref, room_ref, caps1_ref, out_ref):
    days, facilities = caps_ref.shape
    total = in_ref[0]
    for k in range(1, in_ref.shape[0]):
        total = total + in_ref[k]
    uses = days * facilities
    caps = caps_ref[...]
    new = jnp.minimum(caps - ETA * (unflat(total[:, :uses], days) - room_ref[...]), 0.0)
    caps1_ref[...] = new
    gone = new - caps
    primal = total[:, uses : uses + LANES]
    dual = total[:, uses + LANES :] + jnp.sum(folded(gone * gone), axis=0, keepdims=True)
    for k in range(out_ref.shape[0]):
        out_ref[k, :, :LANES] = primal
        out_ref[k, :, LANES:] = dual


def next_duals(w_ref, sum_ref, inflow_ref, gamma_ref, prior_ref, chip_ref, far_ref, w1_ref, kt_ref):
    days, classes = w_ref.shape
    rows = rows_iota((days, LANES))
    second = second_core()
    more = jnp.where(lax.axis_index("day") == lax.axis_size("day") - 1, F32(0.0), F32(ETA))
    for k in range(classes // LANES):
        at = pl.ds(k * LANES, LANES)
        gamma = gamma_ref[:, at]
        sums = sum_ref[:, at]
        prior = jnp.where(rows == 0, prior_ref[:, at], pltpu.roll(sums, 1, 0))
        w = w_ref[:, at] - ETA * (sums - gamma * prior - inflow_ref[:, at])
        w1_ref[:, at] = w
        lead = jnp.where(second, far_ref[:, at], chip_ref[:, at])
        edge = lead + more * (gamma * sums[days - 1 :])
        kt_ref[:, at] = w - gamma * jnp.where(rows == days - 1, edge, pltpu.roll(w, days - 1, 0))


def next_grad(
    cost_hbm, x_hbm, weights_ref, caps_ref, kt_ref, fac_ref, grad_ref, head_ref, sems, head_sem
):
    days, classes = kt_ref.shape
    arrive = block_copies([(cost_hbm, grad_ref)], sems)
    start_all(arrive)
    head = pltpu.make_async_copy(x_hbm.at[:, :, pl.ds(0, BLOCK)], head_ref, head_sem)
    head.start()
    caps = caps_ref[...]
    weights = weights_ref[...]

    def step(j, _):
        for u in range(STEP // LANES):
            at = lanes_of(j, u)
            pulled = pulled_of(caps, fac_ref[:, at])
            for t in range(days):
                grad_ref[t, :, at] = grad_ref[t, :, at] - kt_ref[t : t + 1, at] - weights * pulled[t : t + 1]
        return 0

    each = BLOCK // STEP
    for k, block in enumerate(arrive):
        wait_all(block)
        lax.fori_loop(k * each, (k + 1) * each, step, 0)
    head.wait()


def second_primal(
    x_hbm, x_head, moved_ref, weights_ref, grad_ref, bound_ref, fac_ref, caps_ref,
    x2_hbm, sum_ref, last_hbm, omega_ref, out_hbm,
    x_ref, weighted_ref, last_ref, out_ref, sems, small_sems,
):
    days, classes = sum_ref.shape
    ready = x_head.shape[2] // BLOCK
    arrive = block_copies([(x_hbm, x_ref)], sems, ready)
    leave = block_copies([(x_ref, x2_hbm)], sems.at[1:])
    start_all(arrive)
    total = moved_ref[0]
    for k in range(1, moved_ref.shape[0]):
        total = total + moved_ref[k]
    primal = jnp.sum(total[:, :LANES], axis=1, keepdims=True)
    dual = jnp.sum(total[:, LANES:], axis=1, keepdims=True)
    omega = jnp.sqrt(jnp.sqrt((dual + EPS) / (primal + EPS)))
    omega_ref[...] = jnp.broadcast_to(omega, omega_ref.shape)
    tau = jnp.broadcast_to(ETA / omega, (8, LANES))
    weights = weights_ref[...]

    def step(x_at, j, _):
        for u in range(STEP // LANES):
            at = lanes_of(j, u)
            bound = bound_ref[:, at]
            sums, weighted = [], []
            for t in range(days):
                old = x_at[t, :, at]
                new = jnp.minimum(jnp.maximum(old - tau * grad_ref[t, :, at], 0.0), bound)
                x_ref[t, :, at] = new
                extra = new + (new - old)
                sums.append(extra)
                weighted.append(weights * extra)
            sums = row_sums(sums)
            sum_ref[:, at] = sums
            weighted_ref[:, at] = row_sums(weighted)
            last_ref[:, at] = sums[days - 1 :]
        return 0

    each = BLOCK // STEP
    for k in range(len(leave)):
        if k >= ready:
            wait_all(arrive[k - ready])
        source = x_ref if k >= ready else x_head
        lax.fori_loop(k * each, (k + 1) * each, functools.partial(step, source), 0)
        start_all(leave[k : k + 1])
    row = pltpu.make_async_copy(last_ref, last_hbm, small_sems.at[0])
    row.start()
    blocks = out_ref.shape[0]
    own = caps_ref.shape[1] // blocks
    out_ref[...] = jnp.zeros(out_ref.shape, F32)
    parts = facility_sums(weighted_ref, fac_ref, own * blocks)
    for k in range(blocks):
        g, place = divmod(k * own, WIDE)
        out_ref[k, :, :own] = parts[g][:, place : place + own]
        out_ref[k, :, own : 2 * own] = caps_ref[:, k * own : (k + 1) * own]
    out = pltpu.make_async_copy(out_ref, out_hbm, small_sems.at[1])
    out.start()
    row.wait()
    out.wait()
    for block in leave:
        wait_all(block)


def last_duals(
    in_ref, room_ref, omega_ref, w_ref, sum_ref, prior_ref, inflow_ref, gamma_ref, w2_ref, caps2_ref
):
    days, classes = w_ref.shape
    sigma = ETA * omega_ref[...]
    own = room_ref.shape[1]
    use = in_ref[0, :, :own]
    for k in range(1, in_ref.shape[0]):
        use = use + in_ref[k, :, :own]
    caps2_ref[...] = jnp.minimum(
        in_ref[0, :, own : 2 * own] - sigma[:1, :1] * (use - room_ref[...]), 0.0
    )
    rows = rows_iota((days, LANES))
    for k in range(classes // LANES):
        at = pl.ds(k * LANES, LANES)
        sums = sum_ref[:, at]
        prior = jnp.where(rows == 0, prior_ref[:, at], pltpu.roll(sums, 1, 0))
        w2_ref[:, at] = w_ref[:, at] - sigma * (sums - gamma_ref[:, at] * prior - inflow_ref[:, at])


def to_next(row):
    n = lax.axis_size("day")
    return lax.ppermute(row, "day", [(i, i + 1) for i in range(n - 1)])


def to_previous(row):
    n = lax.axis_size("day")
    return lax.ppermute(row, "day", [(i + 1, i) for i in range(n - 1)])


def swapped(rows, first):
    n = lax.axis_size("day")
    pairs = [(i, i + 1) for i in range(first, n - 1, 2)]
    return lax.ppermute(rows, "day", pairs + [(j, i) for i, j in pairs])


def local(
    cost, x_start, ybal_start, inflow, ycap_start, capacity, upper, facility, option_count,
    decay_index, decay_table, usage,
):
    days, opts, classes = cost.shape
    own = ycap_start.shape[1]
    blocks = lax.axis_size("cls")
    facilities = own * blocks
    fac = facility.reshape(1, classes)
    count = option_count.reshape(1, classes)
    index = decay_index.reshape(1, classes)

    ends, row = call(
        start, "start", [struct(blocks, days, LANES), struct(1, classes)], [ANY] * 3,
        [pltpu.VMEM((days, own), F32), pltpu.VMEM((days, own), F32), pltpu.SemaphoreType.DMA((3,))],
    )(*in_hbm(ycap_start, capacity, ybal_start))
    after = to_previous(row)
    ends = lax.all_to_all(ends, "cls", 0, 0)
    field, rows, row, tile = (
        struct(days, opts, classes), struct(days, classes), struct(1, classes), struct(8, LANES)
    )
    table = struct(days, facilities)
    head = struct(days, opts, HEAD)
    two = struct(2, opts, classes)
    cost_head, x_head, cost_edge, x_edge, kt, w, inflow, bound, fac, gamma, weights = call(
        load, "load",
        [head, head, two, two, rows, rows, rows, struct(opts, classes),
         jax.ShapeDtypeStruct((1, classes), jnp.int32), row, tile],
        [ANY] * 10,
        [pltpu.SMEM((opts,), F32), pltpu.SMEM(decay_table.shape, F32), pltpu.VMEM((1, classes), jnp.int32),
         pltpu.VMEM((1, classes), jnp.int32), pltpu.SemaphoreType.DMA((14,))],
        cost=PASS,
    )(*in_hbm(usage, decay_table, ybal_start, inflow, upper, fac, count, index, cost, x_start))
    streams = classes // BLOCK
    kt, pulled, chip, far, caps, room = call(
        edge_primal, "edge_primal", [rows, rows, row, row, table, table], [VM] * 11
    )(cost_edge, x_edge, weights, ends, after, kt, gamma, w, inflow, bound, fac)
    chip = swapped(chip, 0)
    far = swapped(far, 1)
    x1, sums, moved, use, dual = call(
        first_primal, "first_primal", [pltpu.HBM(field.shape, F32), rows, tile, table, tile],
        [ANY] * 2 + [VM] * 9,
        [pltpu.VMEM(field.shape, F32), pltpu.VMEM(field.shape, F32), pltpu.VMEM(rows.shape, F32),
         pltpu.SemaphoreType.DMA((3, streams))],
        limit=8, out_specs=[ANY] + [VM] * 4, cost=LONG,
    )(*in_hbm(cost, x_start), cost_head, x_head, weights, pulled, kt, bound, inflow, gamma, fac)
    sent, prior = call(
        first_send, "first_send", [struct(blocks, 1, days * facilities + 2 * LANES), row], [VM] * 8
    )(use, moved, dual, chip, far, sums, inflow, gamma)
    got = lax.all_to_all(sent, "cls", 0, 0)
    caps1, sent = call(
        caps_step, "caps_step", [table, struct(lax.axis_size("day"), 1, 2 * LANES)], [VM] * 3
    )(got, caps, room)
    w1, kt = call(next_duals, "next_duals", [rows, rows], [VM] * 7, cost=PASS)(
        w, sums, inflow, gamma, prior, chip, far
    )
    got = lax.all_to_all(sent, "day", 0, 0)
    grad, x1_head = call(
        next_grad, "next_grad", [field, struct(days, opts, BLOCK)], [ANY] * 2 + [VM] * 4,
        [pltpu.SemaphoreType.DMA((1, streams)), pltpu.SemaphoreType.DMA], cost=PASS,
    )(*in_hbm(cost, x1), weights, caps1, kt, fac)
    x2, sums2, last2, omega, sent = call(
        second_primal, "second_primal",
        [pltpu.HBM(field.shape, F32), rows, pltpu.HBM(row.shape, F32), tile,
         pltpu.HBM((blocks, days, LANES), F32)],
        [ANY] + [VM] * 7,
        [pltpu.VMEM(field.shape, F32), pltpu.VMEM(rows.shape, F32), pltpu.VMEM(row.shape, F32),
         pltpu.VMEM((blocks, days, LANES), F32), pltpu.SemaphoreType.DMA((2, streams)),
         pltpu.SemaphoreType.DMA((2,))],
        limit=8, out_specs=[ANY, VM, ANY, VM, ANY],
    )(*in_hbm(x1), x1_head, got, weights, grad, bound, fac, caps1)
    prior2 = to_next(last2)
    got = lax.all_to_all(sent, "cls", 0, 0)
    w2, caps2 = call(last_duals, "last_duals", [struct(days, classes), struct(days, own)], [VM] * 8)(
        got, capacity, omega, w1, sums2, prior2, inflow, gamma
    )
    return x2, w2, caps2


def solution(mesh):
    in_specs = (
        P("day", None, "cls"), P("day", None, "cls"), P("day", "cls"), P("day", "cls"),
        P("day", "cls"), P("day", "cls"), P(None, "cls"), P("cls"), P("cls"), P("cls"), P(), P(),
    )
    out_specs = (P("day", None, "cls"), P("day", "cls"), P("day", "cls"))
    return jax.shard_map(local, mesh=mesh, in_specs=in_specs, out_specs=out_specs, check_vma=False)
```
